32 devices in a mesh: dp: 16 (over z, x, core), seq: 2 (over y).
Axes of the slice: x: 2, y: 2, z: 4, core: 2. Of those that a mesh axis runs over, the one named last changes fastest.
Arguments:
- tokens: bfloat16 [32, 256, 768], P('dp', 'seq'), may hold values from -6 to 6
- pair: bfloat16 [32, 256, 256, 256], P('dp', 'seq'), may hold values from -6 to 6
- cath_class: int32 [32], P('dp'), may hold values from 0 to 4
- cath_arch: int32 [32], P('dp'), may hold values from 0 to 42
- cath_topo: int32 [32], P('dp'), may hold values from 0 to 1471
- times: float32 [32], P('dp'), may hold values from 0.02 to 1
- out_grad: bfloat16 [32, 256, 768], P('dp', 'seq'), may hold values from -6 to 6
- emb_class: bfloat16 [5, 768], P(None, ('dp', 'seq')), may hold values from -4 to 4
- emb_arch: bfloat16 [43, 768], P(None, ('dp', 'seq')), may hold values from -4 to 4
- emb_topo: bfloat16 [1472, 768], P(None, ('dp', 'seq')), may hold values from -4 to 4
- w_time: bfloat16 [256, 768], P(('dp', 'seq')), may hold values from -0.375 to 0.375
- w_ada: bfloat16 [768, 4608], P(('dp', 'seq')), may hold values from -0.21875 to 0.21875
- w_qkv: bfloat16 [768, 2304], P(('dp', 'seq')), may hold values from -0.21875 to 0.21875
- w_gate: bfloat16 [768, 768], P(('dp', 'seq')), may hold values from -0.21875 to 0.21875
- w_out: bfloat16 [768, 768], P(('dp', 'seq')), may hold values from -0.875 to 0.875
- w_pair: bfloat16 [256, 12], P(('dp', 'seq')), may hold values from -0.375 to 0.375
- w_ffgate: bfloat16 [768, 3072], P(('dp', 'seq')), may hold values from -0.21875 to 0.21875
- w_ffup: bfloat16 [768, 3072], P(('dp', 'seq')), may hold values from -0.21875 to 0.21875
- w_ffdown: bfloat16 [3072, 768], P(('dp', 'seq')), may hold values from -0.109375 to 0.109375
Outputs:
- output: bfloat16 [32, 256, 768], P('dp', 'seq')
- input_grad: bfloat16 [32, 256, 768], P('dp', 'seq')
- pair_grad: bfloat16 [32, 256, 256, 256], P('dp', 'seq')
- grad_emb_class: float32 [5, 768], P(None, ('dp', 'seq'))
- grad_emb_arch: float32 [43, 768], P(None, ('dp', 'seq'))
- grad_emb_topo: float32 [1472, 768], P(None, ('dp', 'seq'))
- grad_w_time: float32 [256, 768], P(('dp', 'seq'))
- grad_w_ada: float32 [768, 4608], P(('dp', 'seq'))
- grad_w_qkv: float32 [768, 2304], P(('dp', 'seq'))
- grad_w_gate: float32 [768, 768], P(('dp', 'seq'))
- grad_w_out: float32 [768, 768], P(('dp', 'seq'))
- grad_w_pair: float32 [256, 12], P(('dp', 'seq'))
- grad_w_ffgate: float32 [768, 3072], P(('dp', 'seq'))
- grad_w_ffup: float32 [768, 3072], P(('dp', 'seq'))
- grad_w_ffdown: float32 [3072, 768], P(('dp', 'seq'))
The draws below stay inside these ranges and needn't reach their ends.
All inputs are finite; a program needn't handle non-finite values.
Results may differ from the reference program's by a relative error of at most 0.017.
The reference program's roundings to bfloat16 on the way count: a program that leaves them out, or rounds other values in their place, can miss the bound.
Values may be sent and summed in bfloat16 or wider, within the bound.
No kernel may reach another device: no remote copies, remote signals or barrier semaphores. Data moves between devices by JAX's collectives and lax.ppermute only.
A program may use at most 256 MiB of HBM per device.

```python
import math
import jax
import jax.numpy as jnp
from jax import lax

D = 768
H = 12
FF = 3072
PAIRC = 256
TIMEF = 256
NCLASS = 5
NARCH = 43
NTOPO = 1472
L = 256
CHAINS = 32


def plant(drawn, key, low, largest):
    longest = drawn.shape.index(max(drawn.shape))
    spots = []
    for shift in (0, 1):
        where = [jax.random.randint(jax.random.fold_in(key, axis), (), 0, length) for axis, length in enumerate(drawn.shape)]
        where[longest] = (where[longest] + shift) % drawn.shape[longest]
        spots.append(tuple(where))
    return drawn.at[spots[0]].set(low).at[spots[1]].set(largest)


def steps_of(rng, shape, cuts, low, top_value):
    level = 1.0
    for dim, blocks in cuts:
        heights = jax.random.uniform(jax.random.fold_in(jax.random.fold_in(rng, 6), dim), (blocks,), jnp.float32, low / len(cuts), top_value / len(cuts))
        level = level * jnp.repeat(jnp.exp(heights), shape[dim] // blocks).reshape((-1,) + (1,) * (len(shape) - 1 - dim))
    return level


def normal_values(rng, shape, scale, limit, pieces=(), kind=jnp.bfloat16):
    loudness = steps_of(rng, shape, pieces, -0.22, 0.18) if pieces else 1.0
    values = jax.random.normal(rng, shape, jnp.float32) * scale * loudness
    return jnp.minimum(jnp.maximum(values, -limit), limit).astype(kind)


def setup_inputs(seed: int = 0) -> dict:
    streams_of = jax.random.split(jax.random.key(seed), 20)
    return {
        "tokens": normal_values(streams_of[0], (CHAINS, L, D), 1.0, 6.0, ((0, 16), (1, 2))),
        "pair": normal_values(streams_of[1], (CHAINS, L, L, PAIRC), 1.0, 6.0, ((0, 16), (1, 2))),
        "cath_class": plant(jax.random.randint(streams_of[2], (CHAINS,), 0, NCLASS), jax.random.fold_in(streams_of[2], 1), 0, NCLASS - 1).astype(jnp.int32),
        "cath_arch": plant(jax.random.randint(streams_of[3], (CHAINS,), 0, NARCH), jax.random.fold_in(streams_of[3], 1), 0, NARCH - 1).astype(jnp.int32),
        "cath_topo": plant(jax.random.randint(streams_of[4], (CHAINS,), 0, NTOPO), jax.random.fold_in(streams_of[4], 1), 0, NTOPO - 1).astype(jnp.int32),
        "times": jnp.clip(0.02 + 0.98 * jax.random.uniform(streams_of[5], (CHAINS,), jnp.float32) ** steps_of(streams_of[5], (CHAINS,), ((0, 16),), -0.2, 0.2), 0.02, 1.0),
        "out_grad": normal_values(streams_of[6], (CHAINS, L, D), 1.0, 6.0, ((0, 16), (1, 2))),
        "emb_class": normal_values(streams_of[7], (NCLASS, D), 0.6, 4.0, ((1, 32),)),
        "emb_arch": normal_values(streams_of[8], (NARCH, D), 0.6, 4.0, ((1, 32),)),
        "emb_topo": normal_values(streams_of[9], (NTOPO, D), 0.6, 4.0, ((1, 32),)),
        "w_time": normal_values(streams_of[10], (TIMEF, D), TIMEF ** -0.5, 0.375, ((0, 32),)),
        "w_ada": normal_values(streams_of[11], (D, 6 * D), D ** -0.5, 0.21875, ((0, 32),)),
        "w_qkv": normal_values(streams_of[12], (D, 3 * D), D ** -0.5, 0.21875, ((0, 32),)),
        "w_gate": normal_values(streams_of[13], (D, D), D ** -0.5, 0.21875, ((0, 32),)),
        "w_out": normal_values(streams_of[14], (D, D), (D // 16) ** -0.5, 0.875, ((0, 32),)),
        "w_pair": normal_values(streams_of[15], (PAIRC, H), PAIRC ** -0.5, 0.375, ((0, 32),)),
        "w_ffgate": normal_values(streams_of[16], (D, FF), D ** -0.5, 0.21875, ((0, 32),)),
        "w_ffup": normal_values(streams_of[17], (D, FF), D ** -0.5, 0.21875, ((0, 32),)),
        "w_ffdown": normal_values(streams_of[18], (FF, D), FF ** -0.5, 0.109375, ((0, 32),)),
    }


EPSILON = 1e-06
TIME_SCALE = 100.0

@jax.custom_vjp
def low(v):
    return lax.optimization_barrier(v.astype(jnp.bfloat16)).astype(jnp.float32)

@jax.custom_vjp
def low_back(v):
    return v

def low_keep(v):
    return (low(v), None)

def low_pass(kept, grad):
    return (grad,)

def back_keep(v):
    return (v, None)

def back_low(kept, grad):
    return (low(grad),)
low.defvjp(low_keep, low_pass)
low_back.defvjp(back_keep, back_low)

def matmul(left, right):
    return jnp.dot(left, right, precision=lax.Precision.HIGHEST)

def modulate(rows, shift, scale):
    centre = rows - lax.optimization_barrier(jnp.mean(rows, axis=-1, keepdims=True))
    spread = lax.optimization_barrier(jnp.mean(centre * centre, axis=-1, keepdims=True))
    return centre * lax.rsqrt(spread + EPSILON) * (1.0 + scale) + shift

def time_features(moment, width):
    half_width = width // 2
    frequency = jnp.exp(-math.log(10000.0) * jnp.arange(half_width, dtype=jnp.float32) / half_width)
    angles = TIME_SCALE * moment[:, None] * frequency[None, :]
    return jnp.concatenate([jnp.sin(angles), jnp.cos(angles)], axis=-1)

def chain_forward(params, rows, pair_rows, hot_class, hot_arch, hot_topo, moment):
    emb_class, emb_arch, emb_topo, w_time, w_ada, w_qkv, w_gate, w_out, w_pair, w_ffgate, w_ffup, w_ffdown = params
    width = rows.shape[-1]
    length = rows.shape[0]
    heads = w_pair.shape[1]
    head_size = width // heads
    factor = head_size ** (-0.5)
    features = low(time_features(moment[None], w_time.shape[0]))
    before = matmul(hot_class[None], emb_class) + matmul(hot_arch[None], emb_arch) + matmul(hot_topo[None], emb_topo) + matmul(features, w_time)
    condition = jax.nn.silu(before)
    modes = matmul(low(condition), w_ada)
    shift_one, scale_one, gate_one, shift_two, scale_two, gate_two = jnp.split(modes, 6, axis=-1)
    normed_one = low(modulate(rows, shift_one, scale_one))
    projected = low(low_back(matmul(normed_one, w_qkv)))
    gate_logits = low_back(matmul(normed_one, w_gate))
    queries = projected[:, :width].reshape(length, heads, head_size)
    keys = projected[:, width:2 * width].reshape(length, heads, head_size)
    values = projected[:, 2 * width:].reshape(length, heads, head_size)
    bias = jnp.einsum('ijc,ch->hij', pair_rows, w_pair, precision=lax.Precision.HIGHEST)
    scores = low_back(jnp.einsum('ihd,jhd->hij', queries, keys, precision=lax.Precision.HIGHEST) * factor + bias)
    probs = jax.nn.softmax(scores, axis=-1)
    attended = low_back(jnp.einsum('hij,jhd->ihd', low(probs), values, precision=lax.Precision.HIGHEST).reshape(length, width))
    gated = low(attended * jax.nn.sigmoid(gate_logits))
    branch_one = low_back(matmul(gated, w_out))
    middle = rows + gate_one * branch_one
    normed_two = low(modulate(middle, shift_two, scale_two))
    ff_gate = low_back(matmul(normed_two, w_ffgate))
    ff_up = low_back(matmul(normed_two, w_ffup))
    hidden = low(jax.nn.silu(ff_gate) * ff_up)
    branch_two = low_back(matmul(hidden, w_ffdown))
    return middle + gate_two * branch_two

def reference(tokens, pair, cath_class, cath_arch, cath_topo, times, out_grad, emb_class, emb_arch, emb_topo, w_time, w_ada, w_qkv, w_gate, w_out, w_pair, w_ffgate, w_ffup, w_ffdown):
    params = (emb_class.astype(jnp.float32), emb_arch.astype(jnp.float32), emb_topo.astype(jnp.float32), w_time.astype(jnp.float32), w_ada.astype(jnp.float32), w_qkv.astype(jnp.float32), w_gate.astype(jnp.float32), w_out.astype(jnp.float32), w_pair.astype(jnp.float32), w_ffgate.astype(jnp.float32), w_ffup.astype(jnp.float32), w_ffdown.astype(jnp.float32))
    hot_class = (cath_class[:, None] == jnp.arange(NCLASS, dtype=jnp.int32)[None, :]).astype(jnp.float32)
    hot_arch = (cath_arch[:, None] == jnp.arange(NARCH, dtype=jnp.int32)[None, :]).astype(jnp.float32)
    hot_topo = (cath_topo[:, None] == jnp.arange(NTOPO, dtype=jnp.int32)[None, :]).astype(jnp.float32)
    chain_fn = jax.checkpoint(chain_forward)

    def forward(weights, rows_all, pair_all):

        def advance(carry, entry):
            return (carry, chain_fn(weights, *entry))
        _, result = lax.scan(advance, jnp.zeros((), jnp.float32), (rows_all, pair_all, hot_class, hot_arch, hot_topo, times))
        return result
    result, backward = jax.vjp(forward, params, tokens.astype(jnp.float32), pair.astype(jnp.float32))
    grads, tokens_grad, pairs_grad = backward(out_grad.astype(jnp.float32))
    return (result.astype(jnp.bfloat16), tokens_grad.astype(jnp.bfloat16), pairs_grad.astype(jnp.bfloat16), grads[0], grads[1], grads[2], grads[3], grads[4], grads[5], grads[6], grads[7], grads[8], grads[9], grads[10], grads[11])
```

```python
import math

import jax
import jax.numpy as jnp
from jax import lax
from jax.sharding import Mesh
from jax.sharding import PartitionSpec as P

EPSILON = 1e-06
TIME_SCALE = 100.0
F32 = jnp.float32
BF16 = jnp.bfloat16
DP = ("z", "x", "c")
ALL = ("z", "x", "c", "y")
HIGH = lax.Precision.HIGHEST


def dot(left, right, dims=((1,), (0,))):
    return lax.dot_general(left, right, (dims, ((), ())), preferred_element_type=F32)


def time_features(moment, width):
    half_width = width // 2
    frequency = jnp.exp(-math.log(10000.0) * jnp.arange(half_width, dtype=F32) / half_width)
    angles = TIME_SCALE * moment[:, None] * frequency[None, :]
    return jnp.concatenate([jnp.sin(angles), jnp.cos(angles)], axis=-1)


def normalise(rows):
    centre = rows - jnp.mean(rows, axis=-1, keepdims=True)
    spread = jnp.mean(centre * centre, axis=-1, keepdims=True)
    root = lax.rsqrt(spread + EPSILON)
    return centre * root, root


def normalise_back(grad, scale, normed, root):
    u = grad * (1.0 + scale)
    inner = u - jnp.mean(u, axis=-1, keepdims=True)
    return root * (inner - normed * jnp.mean(u * normed, axis=-1, keepdims=True))


def swap(value, axis):
    return lax.ppermute(value, axis, [(0, 1), (1, 0)])


def shift(value, axis, size, by):
    return lax.ppermute(value, axis, [(i, (i + by) % size) for i in range(size)])


def add_low(left, right):
    return (left.astype(F32) + right.astype(F32)).astype(BF16)


def reduce_scatter(grad, sizes):
    nz, nx, nc, ny = sizes
    rows, columns = grad.shape[1:]
    here = lax.axis_index("c")
    parts = grad.reshape(nz, nx, nc, ny, rows, columns)
    pick = lambda a, i, axis: lax.dynamic_index_in_dim(a, i, axis, keepdims=False)
    parts = add_low(pick(parts, here, 2), swap(pick(parts, 1 - here, 2), "c"))
    half = rows // 2
    done = []
    for which, order in enumerate((("y", "x"), ("x", "y"))):
        block = parts[:, :, :, which * half : (which + 1) * half]
        left = ["z", "x", "y"]
        for axis in order:
            at = left.index(axis)
            here = lax.axis_index(axis)
            block = add_low(pick(block, here, at), swap(pick(block, 1 - here, at), axis))
            left.remove(axis)
        place = lax.axis_index("z")
        total = pick(block, place, 0).astype(F32)
        for by in range(1, nz):
            total = total + shift(pick(block, (place + by) % nz, 0), "z", nz, by).astype(F32)
        done.append(total)
    return jnp.concatenate(done, axis=0)


def on_device(sizes, tokens, pair, cath_class, cath_arch, cath_topo, times, out_grad,
              emb_class, emb_arch, emb_topo, w_time, w_ada, w_qkv, w_gate, w_out, w_pair,
              w_ffgate, w_ffup, w_ffdown):
    nz, nx, nc, ny = sizes
    ndp = nz * nx * nc
    devices = ndp * ny
    chains, local, width = tokens.shape
    length = pair.shape[2]
    heads = w_pair.shape[1]
    head = width // heads
    factor = head ** (-0.5)
    rows = chains * local
    own = emb_class.shape[1]
    hidden_width = w_ffgate.shape[1]
    time_rows = w_time.shape[0]

    attention_w = lax.all_gather(jnp.concatenate([w_qkv, w_gate, w_out], axis=1), ALL, axis=0, tiled=True)
    full_qkv_gate = attention_w[:, : 4 * width]
    full_qkv = attention_w[:, : 3 * width]
    full_gate = attention_w[:, 3 * width : 4 * width]
    full_out = attention_w[:, 4 * width :]
    full_ff = lax.all_gather(jnp.concatenate([w_ffgate, w_ffup], axis=1), ALL, axis=0, tiled=True)
    full_down = lax.all_gather(w_ffdown, ALL, axis=0, tiled=True)

    facts = jnp.stack([cath_class.astype(F32), cath_arch.astype(F32), cath_topo.astype(F32), times]).reshape(1, -1)
    pair_rows_w = w_pair.astype(F32).reshape(1, -1)
    pack = jnp.concatenate(
        [
            w_time.astype(F32).reshape(time_rows, devices, own).transpose(1, 0, 2).reshape(devices, -1),
            jnp.broadcast_to(facts, (devices, facts.shape[1])),
            jnp.broadcast_to(pair_rows_w, (devices, pair_rows_w.shape[1])),
        ],
        axis=1,
    )
    got = lax.all_to_all(pack, ALL, split_axis=0, concat_axis=0, tiled=True)
    size_time = time_rows * own
    time_columns = got[:, :size_time].reshape(devices * time_rows, own).astype(BF16)
    size_facts = 4 * chains
    everyone = got[:, size_time : size_time + size_facts].reshape(ndp, ny, 4, chains)[:, 0]
    everyone = everyone.transpose(1, 0, 2).reshape(4, ndp * chains)
    full_pair_w = got[:, size_time + size_facts :].reshape(-1, heads).astype(BF16)
    labels = everyone[:3].astype(jnp.int32)
    features = time_features(everyone[3], devices * time_rows).astype(BF16)
    hot = [
        (labels[k][:, None] == jnp.arange(table.shape[0], dtype=jnp.int32)[None, :]).astype(BF16)
        for k, table in enumerate((emb_class, emb_arch, emb_topo))
    ]
    before = dot(hot[0], emb_class) + dot(hot[1], emb_arch) + dot(hot[2], emb_topo) + dot(features, time_columns)
    sig_before = jax.nn.sigmoid(before)
    condition_low = (before * sig_before).astype(BF16)
    modes_part = dot(condition_low, w_ada)
    modes = lax.all_to_all(modes_part.reshape(ndp, chains, 6 * width), DP, split_axis=0, concat_axis=0, tiled=True)
    modes = jnp.sum(modes, axis=0)
    modes = modes + swap(modes, "y")
    shift_one, scale_one, gate_one, shift_two, scale_two, gate_two = (
        m[:, None, :] for m in jnp.split(modes, 6, axis=-1)
    )

    entry = tokens.astype(F32)
    norm_one, root_one = normalise(entry)
    normed_one = (norm_one * (1.0 + scale_one) + shift_one).astype(BF16).reshape(rows, width)
    everything = dot(normed_one, full_qkv_gate)
    projected = everything[:, : 3 * width].astype(BF16)
    gate_logits = everything[:, 3 * width :]
    queries = projected[:, :width].reshape(chains, local, heads, head)
    mine = projected[:, width:].reshape(chains, local, 2 * width)
    other = swap(mine, "y")
    place = lax.axis_index("y")
    both = jnp.where(place == 0, jnp.concatenate([mine, other], axis=1), jnp.concatenate([other, mine], axis=1))
    keys = both[:, :, :width].reshape(chains, length, heads, head)
    values = both[:, :, width:].reshape(chains, length, heads, head)
    bias = jnp.einsum("bijc,ch->bhij", pair, full_pair_w, preferred_element_type=F32)
    scores = jnp.einsum("bihd,bjhd->bhij", queries, keys, preferred_element_type=F32) * factor + bias
    probs = jax.nn.softmax(scores, axis=-1)
    probs_low = probs.astype(BF16)
    attended = jnp.einsum("bhij,bjhd->bihd", probs_low, values, preferred_element_type=F32).reshape(rows, width)
    sigmoid_gate = jax.nn.sigmoid(gate_logits)
    gated = (attended * sigmoid_gate).astype(BF16)
    branch_one = dot(gated, full_out).reshape(chains, local, width)
    middle = entry + gate_one * branch_one
    norm_two, root_two = normalise(middle)
    normed_two = (norm_two * (1.0 + scale_two) + shift_two).astype(BF16).reshape(rows, width)
    ff_both = dot(normed_two, full_ff)
    ff_gate, ff_up = ff_both[:, :hidden_width], ff_both[:, hidden_width:]
    sig_ff = jax.nn.sigmoid(ff_gate)
    silu_ff = ff_gate * sig_ff
    hidden = (silu_ff * ff_up).astype(BF16)
    branch_two = dot(hidden, full_down).reshape(chains, local, width)
    result = (middle + gate_two * branch_two).astype(BF16)

    upstream = out_grad.astype(F32)
    branch_two_grad = (gate_two * upstream).astype(BF16).reshape(rows, width)
    gate_two_grad = jnp.sum(upstream * branch_two, axis=1)
    grad_down = dot(hidden, branch_two_grad, ((0,), (0,))).astype(BF16)
    hidden_grad = dot(branch_two_grad, full_down, ((1,), (1,)))
    ff_gate_grad = (hidden_grad * ff_up * (sig_ff + silu_ff * (1.0 - sig_ff))).astype(BF16)
    ff_up_grad = (hidden_grad * silu_ff).astype(BF16)
    ff_grad = jnp.concatenate([ff_gate_grad, ff_up_grad], axis=1)
    grad_ff = dot(normed_two, ff_grad, ((0,), (0,))).astype(BF16)
    normed_two_grad = dot(ff_grad, full_ff, ((1,), (1,))).reshape(chains, local, width)
    shift_two_grad = jnp.sum(normed_two_grad, axis=1)
    scale_two_grad = jnp.sum(normed_two_grad * norm_two, axis=1)
    middle_grad = upstream + normalise_back(normed_two_grad, scale_two, norm_two, root_two)
    gate_one_grad = jnp.sum(middle_grad * branch_one, axis=1)
    branch_one_grad = (gate_one * middle_grad).astype(BF16).reshape(rows, width)
    grad_out = dot(gated, branch_one_grad, ((0,), (0,))).astype(BF16)
    gated_grad = dot(branch_one_grad, full_out, ((1,), (1,)))
    attended_grad = (gated_grad * sigmoid_gate).astype(BF16).reshape(chains, local, heads, head)
    logits_grad = (gated_grad * attended * (sigmoid_gate * (1.0 - sigmoid_gate))).astype(BF16)
    value_grad = jnp.einsum("bhij,bihd->bjhd", probs_low, attended_grad, preferred_element_type=F32)
    probs_grad = jnp.einsum("bihd,bjhd->bhij", attended_grad, values, preferred_element_type=F32)
    scores_grad = (probs * (probs_grad - jnp.sum(probs_grad * probs, axis=-1, keepdims=True))).astype(BF16)
    query_grad = jnp.einsum("bhij,bjhd->bihd", scores_grad, keys, preferred_element_type=F32) * factor
    query_grad = query_grad.reshape(rows, width).astype(BF16)
    key_grad = jnp.einsum("bhij,bihd->bjhd", scores_grad, queries, preferred_element_type=F32) * factor
    joined = jnp.concatenate(
        [key_grad.reshape(chains, length, width), value_grad.reshape(chains, length, width)], axis=2
    ).astype(BF16)
    joined = joined.reshape(chains, ny, local, 2 * width)
    keep = lax.dynamic_index_in_dim(joined, place, 1, keepdims=False)
    give = lax.dynamic_index_in_dim(joined, 1 - place, 1, keepdims=False)
    owned = add_low(keep, swap(give, "y")).reshape(rows, 2 * width)
    everything_grad = jnp.concatenate([query_grad, owned, logits_grad], axis=1)
    pair_grad = jnp.einsum("bhij,ch->bijc", scores_grad, full_pair_w, preferred_element_type=F32).astype(BF16)
    grad_pair_w = jnp.einsum("bijc,bhij->ch", pair, scores_grad, preferred_element_type=F32)
    grad_everything = dot(normed_one, everything_grad, ((0,), (0,))).astype(BF16)
    normed_one_grad = dot(everything_grad, full_qkv_gate, ((1,), (1,))).reshape(chains, local, width)
    shift_one_grad = jnp.sum(normed_one_grad, axis=1)
    scale_one_grad = jnp.sum(normed_one_grad * norm_one, axis=1)
    tokens_grad = (middle_grad + normalise_back(normed_one_grad, scale_one, norm_one, root_one)).astype(BF16)

    sum_down = reduce_scatter(grad_down.reshape(devices, -1, width), sizes)
    sum_ff = reduce_scatter(grad_ff.reshape(devices, -1, 2 * hidden_width), sizes)
    sum_attention = reduce_scatter(
        jnp.concatenate([grad_everything, grad_out], axis=1).reshape(devices, -1, 5 * width), sizes
    )

    modes_grad = jnp.concatenate(
        [shift_one_grad, scale_one_grad, gate_one_grad, shift_two_grad, scale_two_grad, gate_two_grad], axis=-1
    )
    modes_grad = modes_grad + swap(modes_grad, "y")
    modes_all = lax.all_to_all(
        jnp.broadcast_to(modes_grad[None], (ndp, chains, 6 * width)), DP, split_axis=0, concat_axis=0, tiled=True
    ).reshape(ndp * chains, 6 * width)
    grad_ada = lax.dot_general(condition_low.astype(F32), modes_all, (((0,), (0,)), ((), ())), precision=HIGH)
    condition_grad = lax.dot_general(modes_all, w_ada.astype(F32), (((1,), (1,)), ((), ())), precision=HIGH)
    before_grad = condition_grad * (sig_before * (1.0 + before * (1.0 - sig_before)))
    outer = lambda left: lax.dot_general(left.astype(F32), before_grad, (((0,), (0,)), ((), ())), precision=HIGH)
    grad_class, grad_arch, grad_topo = outer(hot[0]), outer(hot[1]), outer(hot[2])
    time_pack = jnp.concatenate(
        [outer(features).reshape(devices, time_rows * own), grad_pair_w.reshape(devices, -1)], axis=1
    )
    time_got = lax.all_to_all(time_pack, ALL, split_axis=0, concat_axis=0, tiled=True)
    grad_time = time_got[:, :size_time].reshape(devices, time_rows, own).transpose(1, 0, 2).reshape(time_rows, width)
    grad_pair_own = jnp.sum(time_got[:, size_time:], axis=0).reshape(w_pair.shape)

    return (
        result,
        tokens_grad,
        pair_grad,
        grad_class,
        grad_arch,
        grad_topo,
        grad_time,
        grad_ada,
        sum_attention[:, : 3 * width],
        sum_attention[:, 3 * width : 4 * width],
        sum_attention[:, 4 * width :],
        grad_pair_own,
        sum_ff[:, :hidden_width],
        sum_ff[:, hidden_width:],
        sum_down,
    )


def solution(mesh):
    ndp, ny = mesh.shape["dp"], mesh.shape["seq"]
    sizes = (ndp // 4, 2, 2, ny)
    fine = Mesh(mesh.devices.reshape(sizes), ALL)
    row, col = P(ALL, None), P(None, ALL)
    in_specs = (P(DP, "y", None), P(DP, "y", None, None), P(DP), P(DP), P(DP), P(DP), P(DP, "y", None)) + (col,) * 3 + (row,) * 9
    out_specs = (P(DP, "y", None), P(DP, "y", None), P(DP, "y", None, None)) + (col,) * 3 + (row,) * 9

    def body(*args):
        return on_device(sizes, *args)

    return jax.shard_map(body, mesh=fine, in_specs=in_specs, out_specs=out_specs, check_vma=False)
```

```python
import functools
import math

import jax
import jax.numpy as jnp
from jax import lax
from jax.experimental import pallas as pl
from jax.experimental.pallas import tpu as pltpu
from jax.sharding import Mesh
from jax.sharding import PartitionSpec as P

EPSILON = 1e-06
TIME_SCALE = 100.0
F32 = jnp.float32
BF16 = jnp.bfloat16
DP = ("z", "x", "c")
ALL = ("z", "x", "c", "y")
HIGH = lax.Precision.HIGHEST
NT, TN = ((1,), (1,)), ((0,), (0,))
TILE = 16
VMEM = 60 * 1024 * 1024


def dot(left, right, dims=((1,), (0,))):
    return lax.dot_general(left, right, (dims, ((), ())), preferred_element_type=F32)


def params():
    return pltpu.CompilerParams(vmem_limit_bytes=VMEM)


def time_features(moment, width):
    half_width = width // 2
    frequency = jnp.exp(-math.log(10000.0) * jnp.arange(half_width, dtype=F32) / half_width)
    angles = TIME_SCALE * moment[:, None] * frequency[None, :]
    return jnp.concatenate([jnp.sin(angles), jnp.cos(angles)], axis=-1)


def normalise(rows):
    centre = rows - jnp.mean(rows, axis=-1, keepdims=True)
    spread = jnp.mean(centre * centre, axis=-1, keepdims=True)
    root = lax.rsqrt(spread + EPSILON)
    return centre * root, root


def normalise_back(grad, scale, normed, root):
    u = grad * (1.0 + scale)
    inner = u - jnp.mean(u, axis=-1, keepdims=True)
    return root * (inner - normed * jnp.mean(u * normed, axis=-1, keepdims=True))


def swap(value, axis):
    return lax.ppermute(value, axis, [(0, 1), (1, 0)])


def shift(value, axis, size, by):
    return lax.ppermute(value, axis, [(i, (i + by) % size) for i in range(size)])


def add_low(left, right):
    return (left.astype(F32) + right.astype(F32)).astype(BF16)


def after(value, *others):
    return lax.optimization_barrier((value, *others))[0]


def ordered(own, other, axis, at):
    low = jnp.stack([own, other], axis=at)
    high = jnp.stack([other, own], axis=at)
    return jnp.where(lax.axis_index(axis) == 0, low, high)


class Gathering:
    def __init__(self, block, nz, routes):
        self.nz, self.routes, self.block = nz, routes, block
        self.got = [shift(block, "z", nz, by) for by in range(1, nz)]

    def first(self):
        nz = self.nz
        parts = [self.block] + self.got
        line = jnp.stack([parts[(nz - 1 - i) % nz] for i in range(2 * nz - 1)])
        full = lax.dynamic_slice_in_dim(line, nz - 1 - lax.axis_index("z"), nz, 0)
        half = full.shape[-1] // 2
        self.full = [full[..., :half], full[..., half:]]
        self.got = [swap(f, r[0]) for f, r in zip(self.full, self.routes)]

    def second(self):
        self.full = [ordered(f, g, r[0], 1) for f, g, r in zip(self.full, self.got, self.routes)]
        self.got = [swap(f, r[1]) for f, r in zip(self.full, self.routes)]

    def third(self):
        self.full = [ordered(f, g, r[1], 2 if r[1] == "y" else 1) for f, g, r in zip(self.full, self.got, self.routes)]
        self.got = [swap(f, "c") for f in self.full]

    def total(self):
        return [ordered(f, g, "c", 2).reshape(-1, f.shape[-1]) for f, g in zip(self.full, self.got)]


def spread(rows, order, nz):
    n = 8 * nz * rows
    new = jnp.arange(n, dtype=jnp.int32)
    part = new // (nz * rows)
    at = {"c": part // 4, order[0]: part // 2 % 2, order[1]: part % 2}
    at = {k: v ^ lax.axis_index(k) for k, v in at.items()}
    old = (((new // rows % nz * 2 + at["x"]) * 2 + at["c"]) * 2 + at["y"]) * rows + new % rows
    return (jnp.arange(n, dtype=jnp.int32)[:, None] == old[None, :]).astype(BF16)


def relative(value, hot):
    return dot(hot, value, ((0,), (1,))).astype(BF16)


class Reduction:
    def __init__(self, keep, send, nz, order):
        self.keep, self.nz, self.order = keep, nz, order
        self.got = swap(send, "c")

    def first(self):
        self.give = add_low(self.keep[2:], self.got[2:])
        self.keep = add_low(self.keep[:2], self.got[:2])
        self.got = swap(self.give, self.order[0])
        return self

    def second(self):
        self.give = add_low(self.keep[1], self.got[1])
        self.keep = add_low(self.keep[0], self.got[0])
        self.got = swap(self.give, self.order[1])
        return self

    def third(self):
        self.give = block = add_low(self.keep, self.got)
        place = lax.axis_index("z")
        pick = lambda i: lax.dynamic_index_in_dim(block, i, 0, keepdims=False)
        self.keep = pick(place)
        self.got = [shift(pick((place + by) % self.nz), "z", self.nz, by) for by in range(1, self.nz)]
        return self

    def total(self):
        total = self.keep.astype(F32)
        for got in self.got:
            total = total + got.astype(F32)
        return total


def bias_kernel(pair_ref, wide_ref, out_ref, table):
    lanes = lax.broadcasted_iota(jnp.int32, wide_ref.shape, 1) % TILE
    channels = wide_ref.shape[0]

    @pl.when((pl.program_id(0) == 0) & (pl.program_id(1) == 0))
    def _():
        wide = wide_ref[...].astype(F32)
        for i in range(TILE):
            table[i * channels : (i + 1) * channels, :] = jnp.where(lanes == i, wide, 0.0).astype(BF16)

    rows = jnp.concatenate([pair_ref[0, i] for i in range(TILE)], axis=1)
    out_ref[0, 0] = dot(rows, table[...]).T


def pair_bias(pair, wide):
    chains, local, length, channels = pair.shape
    blocks, tall = local // TILE, wide.shape[1]
    return pl.pallas_call(
        bias_kernel,
        grid=(chains, blocks),
        in_specs=[
            pl.BlockSpec((1, TILE, length, channels), lambda b, i: (b, i, 0, 0)),
            pl.BlockSpec(wide.shape, lambda b, i: (0, 0)),
        ],
        out_specs=pl.BlockSpec((1, 1, tall, length), lambda b, i: (b, i, 0, 0)),
        out_shape=jax.ShapeDtypeStruct((chains, blocks, tall, length), F32),
        scratch_shapes=[pltpu.VMEM((TILE * channels, tall), BF16)],
        compiler_params=params(),
        cost_estimate=pl.CostEstimate(flops=2 * pair.size * tall, bytes_accessed=2 * pair.size, transcendentals=0),
        name="pair_bias",
    )(pair, wide)


def attend_kernel(factor, bias_ref, q_ref, k_ref, v_ref, mask_ref, probs_ref, out_ref):
    heads = mask_ref.shape[0] // TILE
    keys, values, mask = k_ref[0], v_ref[0], mask_ref[...]
    for n in range(bias_ref.shape[1]):
        at = pl.ds(n * TILE, TILE)
        wide = jnp.concatenate([q_ref[at, :]] * heads, axis=0) * mask
        scores = dot(wide, keys, NT) * factor + bias_ref[0, n]
        powers = jnp.exp(scores - jnp.max(scores, axis=-1, keepdims=True))
        probs = powers * (1.0 / jnp.sum(powers, axis=-1, keepdims=True))
        probs_ref[0, n] = probs
        mixed = dot(probs.astype(BF16), values) * mask.astype(F32)
        total = mixed[:TILE]
        for h in range(1, heads):
            total = total + mixed[h * TILE : (h + 1) * TILE]
        out_ref[at, :] = total


def attend(bias, queries, keys, values, mask, factor, group=4):
    chains, blocks, tall, length = bias.shape
    width = mask.shape[1]
    rows = chains * blocks * TILE
    steps = blocks // group
    row_spec = pl.BlockSpec((group * TILE, width), lambda b, i: (b * steps + i, 0))
    square = pl.BlockSpec((1, group, tall, length), lambda b, i: (b, i, 0, 0))
    return pl.pallas_call(
        functools.partial(attend_kernel, factor),
        grid=(chains, steps),
        in_specs=[
            square,
            row_spec,
            pl.BlockSpec((1, length, width), lambda b, i: (b, 0, 0)),
            pl.BlockSpec((1, length, width), lambda b, i: (b, 0, 0)),
            pl.BlockSpec(mask.shape, lambda b, i: (0, 0)),
        ],
        out_specs=[square, row_spec],
        out_shape=[jax.ShapeDtypeStruct(bias.shape, F32), jax.ShapeDtypeStruct((rows, width), F32)],
        compiler_params=params(),
        cost_estimate=pl.CostEstimate(flops=4 * bias.size * width, bytes_accessed=10 * bias.size, transcendentals=bias.size),
        name="attend",
    )(bias, queries, keys, values, mask)


def attend_back_kernel(factor, probs_ref, q_ref, g_ref, k_ref, v_ref, mask_ref, ds_ref, dq_ref, dk_ref, dv_ref, dk_sum, dv_sum):
    heads = mask_ref.shape[0] // TILE
    keys, values, mask = k_ref[0], v_ref[0], mask_ref[...]

    @pl.when(pl.program_id(1) == 0)
    def _():
        dk_sum[...] = jnp.zeros_like(dk_sum)
        dv_sum[...] = jnp.zeros_like(dv_sum)

    for n in range(probs_ref.shape[1]):
        at = pl.ds(n * TILE, TILE)
        probs = probs_ref[0, n]
        queries = jnp.concatenate([q_ref[at, :]] * heads, axis=0) * mask
        grads = jnp.concatenate([g_ref[at, :]] * heads, axis=0) * mask
        probs_grad = dot(grads, values, NT)
        inner = jnp.sum(probs_grad * probs, axis=-1, keepdims=True)
        scores_grad = (probs * (probs_grad - inner)).astype(BF16)
        ds_ref[0, n] = scores_grad
        mixed = dot(scores_grad, keys) * mask.astype(F32)
        total = mixed[:TILE]
        for h in range(1, heads):
            total = total + mixed[h * TILE : (h + 1) * TILE]
        dq_ref[at, :] = (total * factor).astype(BF16)
        dk_sum[...] += dot(scores_grad, queries, TN)
        dv_sum[...] += dot(probs.astype(BF16), grads, TN)

    @pl.when(pl.program_id(1) == pl.num_programs(1) - 1)
    def _():
        dk_ref[0] = (dk_sum[...] * factor).astype(BF16)
        dv_ref[0] = dv_sum[...].astype(BF16)


def attend_back(probs, queries, grads, keys, values, mask, factor, group=4):
    chains, blocks, tall, length = probs.shape
    width = mask.shape[1]
    rows = chains * blocks * TILE
    steps = blocks // group
    row_spec = pl.BlockSpec((group * TILE, width), lambda b, i: (b * steps + i, 0))
    square = pl.BlockSpec((1, group, tall, length), lambda b, i: (b, i, 0, 0))
    return pl.pallas_call(
        functools.partial(attend_back_kernel, factor),
        grid=(chains, steps),
        in_specs=[
            square,
            row_spec,
            row_spec,
            pl.BlockSpec((1, length, width), lambda b, i: (b, 0, 0)),
            pl.BlockSpec((1, length, width), lambda b, i: (b, 0, 0)),
            pl.BlockSpec(mask.shape, lambda b, i: (0, 0)),
        ],
        out_specs=[square, row_spec] + [pl.BlockSpec((1, length, width), lambda b, i: (b, 0, 0))] * 2,
        out_shape=[
            jax.ShapeDtypeStruct(probs.shape, BF16),
            jax.ShapeDtypeStruct((rows, width), BF16),
            jax.ShapeDtypeStruct((chains, length, width), BF16),
            jax.ShapeDtypeStruct((chains, length, width), BF16),
        ],
        scratch_shapes=[pltpu.VMEM((length, width), F32), pltpu.VMEM((length, width), F32)],
        compiler_params=params(),
        cost_estimate=pl.CostEstimate(flops=10 * probs.size * width, bytes_accessed=6 * probs.size, transcendentals=0),
        name="attend_back",
    )(probs, queries, grads, keys, values, mask)


def pair_back_kernel(ds_ref, pair_ref, tall_ref, turn_ref, old_dw_ref, *rest):
    grad_ref, dw_ref, table = rest[-3:]
    channels = tall_ref.shape[1]

    @pl.when(pl.program_id(0) == 0)
    def _():
        rows = lax.broadcasted_iota(jnp.int32, tall_ref.shape, 0) % TILE
        tall = tall_ref[...].astype(F32)
        for i in range(TILE):
            table[:, i * channels : (i + 1) * channels] = jnp.where(rows == i, tall, 0.0).astype(BF16)
        dw_ref[...] = old_dw_ref[...]

    scores_grad = ds_ref[0, 0]
    turned = scores_grad.T
    by_row = dot(turn_ref[...], scores_grad).astype(BF16)
    span = 4
    total = dw_ref[...]
    for k in range(TILE // span):
        spread = dot(turned, table[:, k * span * channels : (k + 1) * span * channels]).astype(BF16)
        for n in range(span):
            i = k * span + n
            grad_ref[0, i] = spread[:, n * channels : (n + 1) * channels]
            total = total + dot(by_row[i * TILE : (i + 1) * TILE], pair_ref[0, i])
    dw_ref[...] = total


def pair_back(scores_grad, pair, tall, turn, part, parts, old_dw, *old):
    chains, local, length, channels = pair.shape
    blocks, high = scores_grad.shape[1:3]
    count = chains * blocks // parts
    place = lambda i: ((part * count + i) // blocks, (part * count + i) % blocks, 0, 0)
    fixed = lambda i: (0, 0)
    return pl.pallas_call(
        pair_back_kernel,
        grid=(count,),
        in_specs=[
            pl.BlockSpec((1, 1, high, length), place),
            pl.BlockSpec((1, TILE, length, channels), place),
            pl.BlockSpec(tall.shape, fixed),
            pl.BlockSpec(turn.shape, fixed),
            pl.BlockSpec((TILE, channels), fixed),
        ]
        + [pl.BlockSpec(memory_space=pl.ANY)] * len(old),
        out_specs=[
            pl.BlockSpec((1, TILE, length, channels), place),
            pl.BlockSpec((TILE, channels), fixed),
        ],
        out_shape=[jax.ShapeDtypeStruct(pair.shape, BF16), jax.ShapeDtypeStruct((TILE, channels), F32)],
        input_output_aliases={5: 0} if old else {},
        scratch_shapes=[pltpu.VMEM((high, TILE * channels), BF16)],
        compiler_params=params(),
        cost_estimate=pl.CostEstimate(flops=4 * pair.size * high // parts, bytes_accessed=4 * pair.size // parts, transcendentals=0),
        name="pair_back",
    )(scores_grad, pair, tall, turn, old_dw, *old)


def feed_kernel(rows_ref, turned_ref, g_ref, order_ref, line_ref, gate_ref, up_ref, down_ref,
                out_ref, back_ref, keep_down, send_down, keep_gate, send_gate, keep_up, send_up):
    @pl.when(pl.program_id(0) == 0)
    def _():
        out_ref[...] = jnp.zeros_like(out_ref)
        back_ref[...] = jnp.zeros_like(back_ref)

    rows, grads = rows_ref[...], g_ref[...]
    w_gate, w_up = gate_ref[...], up_ref[...]
    width = rows.shape[1]
    stack = [down_ref[:, k * width : (k + 1) * width] for k in range(down_ref.shape[1] // width)]
    w_down = dot(line_ref[...], jnp.concatenate(stack, axis=0)).astype(BF16)
    gate = dot(rows, w_gate)
    up = dot(rows, w_up)
    sig = jax.nn.sigmoid(gate)
    silu = gate * sig
    hidden = (silu * up).astype(BF16)
    out_ref[...] += dot(hidden, w_down)
    hidden_grad = dot(grads, w_down, NT)
    gate_grad = (hidden_grad * up * (sig + silu * (1.0 - sig))).astype(BF16)
    up_grad = (hidden_grad * silu).astype(BF16)
    back_ref[...] += dot(gate_grad, w_gate, NT) + dot(up_grad, w_up, NT)
    half = turned_ref.shape[1] // 2
    for k, (right, keep, send) in enumerate(((gate_grad, keep_gate, send_gate), (up_grad, keep_up, send_up))):
        full = dot(turned_ref[k], right).astype(BF16)
        keep[...] = full[:half]
        send[...] = full[half:]
    hidden_turned = dot(order_ref[...], hidden, NT).astype(BF16)
    full = dot(hidden_turned, grads).reshape((2,) + keep_down.shape)
    keep_down[...] = full[0].astype(BF16)
    send_down[...] = full[1].astype(BF16)


def feed(rows, turned, grads, order, line, weights, nz):
    count, width = rows.shape
    hidden = weights.shape[1] // 3
    block = order.shape[0]
    steps = hidden // block
    per = nz // steps
    own = block // (8 * per)
    fixed = lambda m: (0, 0)
    return pl.pallas_call(
        feed_kernel,
        grid=(steps,),
        in_specs=[
            pl.BlockSpec((count, width), fixed),
            pl.BlockSpec((2, width, count), lambda m: (0, 0, 0)),
            pl.BlockSpec((count, width), fixed),
            pl.BlockSpec((block, block), fixed),
            pl.BlockSpec((block, block), fixed),
            pl.BlockSpec((width, block), lambda m: (0, m)),
            pl.BlockSpec((width, block), lambda m: (0, steps + m)),
            pl.BlockSpec((width // steps, hidden), lambda m: (m, 2)),
        ],
        out_specs=[
            pl.BlockSpec((count, width), fixed),
            pl.BlockSpec((count, width), fixed),
            pl.BlockSpec((4, per, own, width), lambda m: (0, m, 0, 0)),
            pl.BlockSpec((4, per, own, width), lambda m: (0, m, 0, 0)),
            *[pl.BlockSpec((width // 2, block), lambda m: (0, m))] * 4,
        ],
        out_shape=[
            jax.ShapeDtypeStruct((count, width), F32),
            jax.ShapeDtypeStruct((count, width), F32),
            jax.ShapeDtypeStruct((4, nz, own, width), BF16),
            jax.ShapeDtypeStruct((4, nz, own, width), BF16),
            *[jax.ShapeDtypeStruct((width // 2, hidden), BF16)] * 4,
        ],
        compiler_params=params(),
        cost_estimate=pl.CostEstimate(flops=24 * count * width * hidden, bytes_accessed=12 * width * hidden, transcendentals=count * hidden),
        name="feed",
    )(rows, turned, grads, order, line, weights, weights, weights)


def join_kernel(*refs):
    at = 0
    for ref in refs[:-1]:
        pieces = [ref[k] for k in range(ref.shape[0])] if len(ref.shape) == 3 else [ref[...]]
        for piece in pieces:
            refs[-1][:, at : at + piece.shape[1]] = piece
            at += piece.shape[1]


def join(*pieces):
    columns = sum(p.shape[-1] * (p.shape[0] if p.ndim == 3 else 1) for p in pieces)
    return pl.pallas_call(
        join_kernel,
        out_shape=jax.ShapeDtypeStruct((pieces[0].shape[-2], columns), BF16),
        compiler_params=params(),
        name="join",
    )(*pieces)


def project_kernel(own_ref, all_ref, first_ref, second_ref, q_ref, k_ref, v_ref, gate_ref):
    width = own_ref.shape[1]
    own, every = own_ref[...], all_ref[...]
    q_ref[...] = dot(own, first_ref[:, :width]).astype(BF16)
    k_ref[...] = dot(every, first_ref[:, width : 2 * width]).astype(BF16)
    v_ref[...] = dot(every, second_ref[:, :width]).astype(BF16)
    gate_ref[...] = dot(own, second_ref[:, width : 2 * width])


def project(own, every, first, second):
    count, width = own.shape
    many = every.shape[0]
    return pl.pallas_call(
        project_kernel,
        out_shape=[
            jax.ShapeDtypeStruct((count, width), BF16),
            jax.ShapeDtypeStruct((many, width), BF16),
            jax.ShapeDtypeStruct((many, width), BF16),
            jax.ShapeDtypeStruct((count, width), F32),
        ],
        compiler_params=params(),
        cost_estimate=pl.CostEstimate(flops=4 * (count + many) * width * width, bytes_accessed=12 * width * width, transcendentals=0),
        name="project",
    )(own, every, first, second)


def project_back_kernel(own_ref, all_ref, gated_ref, dq_ref, dk_ref, dv_ref, dg_ref, out_ref, *sums):
    width = own_ref.shape[1]
    half = width // 2
    for k, (inner, outer) in enumerate((((own_ref, dq_ref), (all_ref, dk_ref)), ((all_ref, dv_ref), (own_ref, dg_ref)))):
        for n in range(2):
            rows = slice(n * half, (n + 1) * half)
            result = sums[2 * k + n]
            result[:, :width] = dot(inner[0][k, rows], inner[1][...]).astype(BF16)
            result[:, width : 2 * width] = dot(outer[0][k, rows], outer[1][...]).astype(BF16)
            result[:, 2 * width :] = dot(gated_ref[k, rows], out_ref[:, k * half : (k + 1) * half]).astype(BF16)


def project_back(own, every, gated, dq, dk, dv, dg, out):
    width = own.shape[1]
    return pl.pallas_call(
        project_back_kernel,
        out_shape=[jax.ShapeDtypeStruct((width // 2, 5 * width // 2), BF16)] * 4,
        compiler_params=params(),
        cost_estimate=pl.CostEstimate(flops=16 * own.size * width, bytes_accessed=16 * width * width, transcendentals=0),
        name="project_back",
    )(own, every, gated, dq, dk, dv, dg, out)


def on_device(sizes, tokens, pair, cath_class, cath_arch, cath_topo, times, out_grad,
              emb_class, emb_arch, emb_topo, w_time, w_ada, w_qkv, w_gate, w_out, w_pair,
              w_ffgate, w_ffup, w_ffdown):
    nz, nx, nc, ny = sizes
    ndp = nz * nx * nc
    devices = ndp * ny
    chains, local, width = tokens.shape
    length = pair.shape[2]
    heads = w_pair.shape[1]
    head = width // heads
    factor = head ** (-0.5)
    rows = chains * local
    own = emb_class.shape[1]
    hidden_width = w_ffgate.shape[1]
    time_rows = w_time.shape[0]

    half = width // 2
    groups = w_ffdown.shape[0] // own
    routes = (("y", "x"), ("x", "y"))
    stacked = join(w_ffgate, w_ffup, w_ffdown.reshape(groups, own, width))
    weights = lax.all_gather(stacked, ALL, axis=0, tiled=True)
    attention = Gathering(
        join(w_qkv[:, : 2 * width], w_out[:, :half], w_qkv[:, 2 * width :], w_gate, w_out[:, half:]), nz, routes
    )
    tokens_other = swap(tokens, "y")

    facts = jnp.stack([cath_class.astype(F32), cath_arch.astype(F32), cath_topo.astype(F32), times]).reshape(1, -1)
    pair_rows_w = w_pair.astype(F32).reshape(1, -1)
    pack = jnp.concatenate(
        [
            w_time.astype(F32).reshape(time_rows, devices, own).transpose(1, 0, 2).reshape(devices, -1),
            jnp.broadcast_to(facts, (devices, facts.shape[1])),
            jnp.broadcast_to(pair_rows_w, (devices, pair_rows_w.shape[1])),
        ],
        axis=1,
    )
    got = lax.all_to_all(pack, ALL, split_axis=0, concat_axis=0, tiled=True)
    size_time = time_rows * own
    time_columns = got[:, :size_time].reshape(devices * time_rows, own).astype(BF16)
    size_facts = 4 * chains
    everyone = got[:, size_time : size_time + size_facts].reshape(ndp, ny, 4, chains)[:, 0]
    everyone = everyone.transpose(1, 0, 2).reshape(4, ndp * chains)
    full_pair_w = got[:, size_time + size_facts :].reshape(-1, heads).astype(BF16)
    labels = everyone[:3].astype(jnp.int32)
    features = time_features(everyone[3], devices * time_rows).astype(BF16)
    hot = [
        (labels[k][:, None] == jnp.arange(table.shape[0], dtype=jnp.int32)[None, :]).astype(BF16)
        for k, table in enumerate((emb_class, emb_arch, emb_topo))
    ]
    before = dot(hot[0], emb_class) + dot(hot[1], emb_arch) + dot(hot[2], emb_topo) + dot(features, time_columns)
    sig_before = jax.nn.sigmoid(before)
    condition_low = (before * sig_before).astype(BF16)
    modes_part = dot(condition_low, w_ada)
    modes = lax.all_to_all(modes_part.reshape(ndp, chains, 6 * width), DP, split_axis=0, concat_axis=0, tiled=True)
    modes = jnp.sum(modes, axis=0)
    modes = modes + swap(modes, "y")
    shift_one, scale_one, gate_one, shift_two, scale_two, gate_two = (
        m[:, None, :] for m in jnp.split(modes, 6, axis=-1)
    )

    entry = tokens.astype(F32)
    norm_one, root_one = normalise(entry)
    normed_one = (norm_one * (1.0 + scale_one) + shift_one).astype(BF16)
    norm_other, _ = normalise(tokens_other.astype(F32))
    normed_other = (norm_other * (1.0 + scale_one) + shift_one).astype(BF16)
    normed_all = ordered(normed_one, normed_other, "y", 1).reshape(chains * length, width)
    normed_one = normed_one.reshape(rows, width)
    mask = (jnp.arange(heads * TILE)[:, None] // TILE == jnp.arange(width)[None, :] // head).astype(BF16)
    wide_pair = jnp.repeat(full_pair_w, TILE, axis=1)
    attention.first()
    bias = pair_bias(after(pair, *attention.full), wide_pair)
    attention.got[0] = after(attention.got[0], bias)
    attention.second()
    hots = [spread(own, route, nz) for route in routes]
    order = spread(groups * own, routes[1], nz * width // hidden_width).T
    in_turned = jnp.stack([relative(normed_one, hot) for hot in hots])
    all_turned = jnp.stack([relative(normed_all, hot) for hot in hots])
    attention.third()
    first_w, second_w = attention.total()
    full_out = jnp.concatenate([first_w[:, 2 * width :], second_w[:, 2 * width :]], axis=1)
    queries, keys, values, gate_logits = project(normed_one, normed_all, first_w, second_w)
    keys, values = keys.reshape(chains, length, width), values.reshape(chains, length, width)
    sigmoid_gate = jax.nn.sigmoid(gate_logits)
    probs, attended = attend(bias, queries, keys, values, mask, factor)
    gated = (attended * sigmoid_gate).astype(BF16)
    branch_one = dot(gated, full_out).reshape(chains, local, width)
    middle = entry + gate_one * branch_one
    norm_two, root_two = normalise(middle)
    normed_two = (norm_two * (1.0 + scale_two) + shift_two).astype(BF16).reshape(rows, width)
    upstream = out_grad.astype(F32)
    branch_two_grad = (gate_two * upstream).astype(BF16).reshape(rows, width)
    out_turned = jnp.stack([relative(gated, hot) for hot in hots])
    turned = jnp.stack([relative(normed_two, hots[k]) for k in (1, 0)])
    steps = hidden_width // width
    new = jnp.arange(width, dtype=jnp.int32)
    per_step = width // (steps * own)
    old = (new // own % groups) * (per_step * own) + new // (groups * own) * own + new % own
    line = (jnp.arange(width, dtype=jnp.int32)[None, :] == old[:, None]).astype(BF16)
    weights = after(weights, out_turned, turned)
    branch_two, normed_two_grad, *grads = feed(normed_two, turned, branch_two_grad, order, line, weights, nz)
    split = lambda v: v.reshape(4, nz, -1, v.shape[-1])
    down_sum = Reduction(grads[0], grads[1], nz, routes[1])
    gate_sum = Reduction(split(grads[2]), split(grads[3]), nz, routes[1])
    up_sum = Reduction(split(grads[4]), split(grads[5]), nz, routes[0])

    normed_two_grad = normed_two_grad.reshape(chains, local, width)
    middle_grad = upstream + normalise_back(normed_two_grad, scale_two, norm_two, root_two)
    branch_one_grad = (gate_one * middle_grad).astype(BF16).reshape(rows, width)
    gated_grad = dot(branch_one_grad, full_out, NT)
    attended_grad = (gated_grad * sigmoid_gate).astype(BF16)
    logits_grad = (gated_grad * attended * (sigmoid_gate * (1.0 - sigmoid_gate))).astype(BF16)
    up_sum.first(), down_sum.first(), gate_sum.first()
    attended_grad = after(attended_grad, down_sum.give, gate_sum.give, up_sum.give)
    scores_grad, query_grad, key_grad, value_grad = attend_back(
        probs, queries, attended_grad, keys, values, mask, factor
    )
    kept_sent = project_back(
        in_turned, all_turned, out_turned, query_grad, key_grad.reshape(-1, width), value_grad.reshape(-1, width),
        logits_grad, branch_one_grad,
    )
    in_sums = [Reduction(split(kept_sent[2 * k]), split(kept_sent[2 * k + 1]), nz, routes[k]) for k in range(2)]
    place = lax.axis_index("y")
    joined = jnp.stack([key_grad, value_grad]).reshape(2, chains, ny, local, width)
    keep = lax.dynamic_index_in_dim(joined, place, 2, keepdims=False)
    give = lax.dynamic_index_in_dim(joined, 1 - place, 2, keepdims=False)
    got = swap(give, "y")
    turn_rows = jnp.arange(TILE * TILE)[:, None]
    turn_columns = jnp.arange(heads * TILE)[None, :]
    turn = ((turn_rows // TILE == turn_columns % TILE) & (turn_rows % TILE == turn_columns // TILE)).astype(BF16)
    tall_pair = wide_pair.T
    pair_sums = (jnp.zeros((TILE, pair.shape[3]), F32),)
    pieces = 4

    def more_pair(k, *needed):
        new_grad, new_sum = pair_back(after(scores_grad, *needed), pair, tall_pair, turn, k, pieces, *pair_sums)
        return (new_sum, new_grad)

    pair_sums = more_pair(0, kept_sent[0])
    up_sum.got = after(up_sum.got, pair_sums[0])
    down_sum.got = after(down_sum.got, pair_sums[0])
    up_sum.second(), down_sum.second()
    for s in in_sums:
        s.got = after(s.got, pair_sums[0])
        s.first()
    pair_sums = more_pair(1, up_sum.give, down_sum.give, *[s.give for s in in_sums])
    owned = add_low(keep, after(got, pair_sums[0])).reshape(2, rows, width)
    gate_sum.got = after(gate_sum.got, pair_sums[0])
    gate_sum.second()
    normed_one_grad = (
        dot(query_grad, first_w[:, :width], NT)
        + dot(owned[0], first_w[:, width : 2 * width], NT)
        + dot(owned[1], second_w[:, :width], NT)
        + dot(logits_grad, second_w[:, width : 2 * width], NT)
    ).reshape(chains, local, width)
    pair_sums = more_pair(2, normed_one_grad, gate_sum.give)
    up_sum.got = after(up_sum.got, pair_sums[0])
    down_sum.got = after(down_sum.got, pair_sums[0])
    up_sum.third(), down_sum.third()
    pair_sums = more_pair(3, up_sum.give, down_sum.give)
    for s in in_sums:
        s.got = after(s.got, pair_sums[0])
        s.second()
    gate_sum.got = after(gate_sum.got, pair_sums[0])
    gate_sum.third()
    for s in in_sums:
        s.third()
    pair_w_sum, pair_grad = pair_sums
    sum_down, sum_gate, sum_up = down_sum.total(), gate_sum.total(), up_sum.total()
    sums = [s.total() for s in in_sums]
    sum_out = jnp.concatenate([s[:, 2 * width :] for s in sums], axis=1)
    grad_pair_w = pair_w_sum[:heads].T

    branch_two = branch_two.reshape(chains, local, width)
    result = (middle + gate_two * branch_two).astype(BF16)
    gate_two_grad = jnp.sum(upstream * branch_two, axis=1)
    shift_two_grad = jnp.sum(normed_two_grad, axis=1)
    scale_two_grad = jnp.sum(normed_two_grad * norm_two, axis=1)
    gate_one_grad = jnp.sum(middle_grad * branch_one, axis=1)
    shift_one_grad = jnp.sum(normed_one_grad, axis=1)
    scale_one_grad = jnp.sum(normed_one_grad * norm_one, axis=1)
    tokens_grad = (middle_grad + normalise_back(normed_one_grad, scale_one, norm_one, root_one)).astype(BF16)

    modes_grad = jnp.concatenate(
        [shift_one_grad, scale_one_grad, gate_one_grad, shift_two_grad, scale_two_grad, gate_two_grad], axis=-1
    )
    modes_grad = modes_grad + swap(modes_grad, "y")
    modes_all = lax.all_to_all(
        jnp.broadcast_to(modes_grad[None], (ndp, chains, 6 * width)), DP, split_axis=0, concat_axis=0, tiled=True
    ).reshape(ndp * chains, 6 * width)
    grad_ada = lax.dot_general(condition_low.astype(F32), modes_all, (((0,), (0,)), ((), ())), precision=HIGH)
    condition_grad = lax.dot_general(modes_all, w_ada.astype(F32), (((1,), (1,)), ((), ())), precision=HIGH)
    before_grad = condition_grad * (sig_before * (1.0 + before * (1.0 - sig_before)))
    outer = lambda left: lax.dot_general(left.astype(F32), before_grad, (((0,), (0,)), ((), ())), precision=HIGH)
    grad_class, grad_arch, grad_topo = outer(hot[0]), outer(hot[1]), outer(hot[2])
    time_pack = jnp.concatenate(
        [outer(features).reshape(devices, time_rows * own), grad_pair_w.reshape(devices, -1)], axis=1
    )
    time_got = lax.all_to_all(time_pack, ALL, split_axis=0, concat_axis=0, tiled=True)
    grad_time = time_got[:, :size_time].reshape(devices, time_rows, own).transpose(1, 0, 2).reshape(time_rows, width)
    grad_pair_own = jnp.sum(time_got[:, size_time:], axis=0).reshape(w_pair.shape)

    return (
        result,
        tokens_grad,
        pair_grad,
        grad_class,
        grad_arch,
        grad_topo,
        grad_time,
        grad_ada,
        jnp.concatenate([sums[0][:, : 2 * width], sums[1][:, :width]], axis=1),
        sums[1][:, width : 2 * width],
        sum_out,
        grad_pair_own,
        sum_gate,
        sum_up,
        sum_down,
    )


def solution(mesh):
    ndp, ny = mesh.shape["dp"], mesh.shape["seq"]
    sizes = (ndp // 4, 2, 2, ny)
    fine = Mesh(mesh.devices.reshape(sizes), ALL)
    row, col = P(ALL, None), P(None, ALL)
    in_specs = (P(DP, "y", None), P(DP, "y", None, None), P(DP), P(DP), P(DP), P(DP), P(DP, "y", None)) + (col,) * 3 + (row,) * 9
    out_specs = (P(DP, "y", None), P(DP, "y", None), P(DP, "y", None, None)) + (col,) * 3 + (row,) * 9

    def body(*args):
        return on_device(sizes, *args)

    return jax.shard_map(body, mesh=fine, in_specs=in_specs, out_specs=out_specs, check_vma=False)
```

```python
import functools
import math

import jax
import jax.numpy as jnp
from jax import lax
from jax.experimental import pallas as pl
from jax.experimental.pallas import tpu as pltpu
from jax.sharding import Mesh
from jax.sharding import PartitionSpec as P

EPSILON = 1e-06
TIME_SCALE = 100.0
F32 = jnp.float32
BF16 = jnp.bfloat16
DP = ("z", "x", "c")
ALL = ("z", "x", "c", "y")
HIGH = lax.Precision.HIGHEST
NT, TN = ((1,), (1,)), ((0,), (0,))
TILE = 16
VMEM = 60 * 1024 * 1024


def dot(left, right, dims=((1,), (0,))):
    return lax.dot_general(left, right, (dims, ((), ())), preferred_element_type=F32)


def params():
    return pltpu.CompilerParams(vmem_limit_bytes=VMEM)


def time_features(moment, width):
    half_width = width // 2
    frequency = jnp.exp(-math.log(10000.0) * jnp.arange(half_width, dtype=F32) / half_width)
    angles = TIME_SCALE * moment[:, None] * frequency[None, :]
    return jnp.concatenate([jnp.sin(angles), jnp.cos(angles)], axis=-1)


def normalise(rows):
    centre = rows - jnp.mean(rows, axis=-1, keepdims=True)
    spread = jnp.mean(centre * centre, axis=-1, keepdims=True)
    root = lax.rsqrt(spread + EPSILON)
    return centre * root, root


def normalise_back(grad, scale, normed, root):
    u = grad * (1.0 + scale)
    inner = u - jnp.mean(u, axis=-1, keepdims=True)
    return root * (inner - normed * jnp.mean(u * normed, axis=-1, keepdims=True))


def swap(value, axis):
    return lax.ppermute(value, axis, [(0, 1), (1, 0)])


def shift(value, axis, size, by):
    return lax.ppermute(value, axis, [(i, (i + by) % size) for i in range(size)])


def add_low(left, right):
    return (left.astype(F32) + right.astype(F32)).astype(BF16)


def after(value, *others):
    return lax.optimization_barrier((value, *others))[0]


def ordered(own, other, axis, at):
    low = jnp.stack([own, other], axis=at)
    high = jnp.stack([other, own], axis=at)
    return jnp.where(lax.axis_index(axis) == 0, low, high)


class Gathering:
    def __init__(self, block, nz, routes):
        self.nz, self.routes, self.block = nz, routes, block
        self.got = [shift(block, "z", nz, by) for by in range(1, nz)]

    def first(self):
        nz = self.nz
        parts = [self.block] + self.got
        line = jnp.stack([parts[(nz - 1 - i) % nz] for i in range(2 * nz - 1)])
        full = lax.dynamic_slice_in_dim(line, nz - 1 - lax.axis_index("z"), nz, 0)
        half = full.shape[-1] // 2
        self.full = [full[..., :half], full[..., half:]]
        self.got = [swap(f, r[0]) for f, r in zip(self.full, self.routes)]

    def second(self):
        self.full = [ordered(f, g, r[0], 1) for f, g, r in zip(self.full, self.got, self.routes)]
        self.got = [swap(f, r[1]) for f, r in zip(self.full, self.routes)]

    def third(self):
        self.full = [ordered(f, g, r[1], 2 if r[1] == "y" else 1) for f, g, r in zip(self.full, self.got, self.routes)]
        self.got = [swap(f, "c") for f in self.full]

    def total(self):
        return [ordered(f, g, "c", 2).reshape(-1, f.shape[-1]) for f, g in zip(self.full, self.got)]


def spread(rows, order, nz):
    n = 8 * nz * rows
    new = jnp.arange(n, dtype=jnp.int32)
    part = new // (nz * rows)
    at = {"c": part // 4, order[0]: part // 2 % 2, order[1]: part % 2}
    at = {k: v ^ lax.axis_index(k) for k, v in at.items()}
    old = (((new // rows % nz * 2 + at["x"]) * 2 + at["c"]) * 2 + at["y"]) * rows + new % rows
    return (jnp.arange(n, dtype=jnp.int32)[:, None] == old[None, :]).astype(BF16)


def down_order(rows, groups, routes, nz):
    n = 8 * nz * rows * groups
    new = jnp.arange(n, dtype=jnp.int32)
    group = new // (8 * nz * rows)
    part = new // (nz * rows) % 8
    late = group >= groups // 2
    firsts, seconds = part // 2 % 2, part % 2
    at = {"c": part // 4}
    for axis in ("x", "y"):
        early_bit = firsts if routes[1][0] == axis else seconds
        late_bit = firsts if routes[0][0] == axis else seconds
        at[axis] = jnp.where(late, late_bit, early_bit)
    at = {k: v ^ lax.axis_index(k) for k, v in at.items()}
    old = (((new // rows % nz * 2 + at["x"]) * 2 + at["c"]) * 2 + at["y"]) * groups * rows + group * rows + new % rows
    return (jnp.arange(n, dtype=jnp.int32)[None, :] == old[:, None]).astype(BF16)


def relative(value, hot):
    return dot(hot, value, ((0,), (1,))).astype(BF16)


class Reduction:
    def __init__(self, keep, send, nz, order):
        self.keep = keep if isinstance(keep, tuple) else (keep[:2], keep[2:])
        self.nz, self.order = nz, order
        self.got = swap(send, "c")

    def first(self):
        self.give = add_low(self.keep[1], self.got[2:])
        self.keep = add_low(self.keep[0], self.got[:2])
        self.got = swap(self.give, self.order[0])
        return self

    def second(self):
        self.give = add_low(self.keep[1], self.got[1])
        self.keep = add_low(self.keep[0], self.got[0])
        self.got = swap(self.give, self.order[1])
        return self

    def third(self):
        return add_low(self.keep, self.got)


class Line:
    def __init__(self, blocks, nz):
        block = jnp.concatenate(blocks, axis=-1)
        place = lax.axis_index("z")
        pick = lambda i: lax.dynamic_index_in_dim(block, i, 0, keepdims=False)
        self.keep = pick(place)
        self.sent = [pick((place + by) % nz) for by in range(1, nz)]
        self.got = [shift(sent, "z", nz, by) for by, sent in enumerate(self.sent, 1)]

    def total(self, *needed):
        total = self.keep.astype(F32)
        for got in after(self.got, *needed):
            total = total + got.astype(F32)
        return total


def bias_kernel(pair_ref, wide_ref, out_ref):
    wide = wide_ref[...]
    lanes = lax.broadcasted_iota(jnp.int32, (pair_ref.shape[2], wide.shape[1]), 1) % TILE
    for n in range(out_ref.shape[1]):
        total = dot(pair_ref[0, n * TILE], wide)
        for i in range(1, TILE):
            total = jnp.where(lanes == i, dot(pair_ref[0, n * TILE + i], wide), total)
        out_ref[0, n] = total.T


def pair_bias(pair, wide, group=4):
    chains, local, length, channels = pair.shape
    blocks, tall = local // TILE, wide.shape[1]
    return pl.pallas_call(
        bias_kernel,
        grid=(chains, blocks // group),
        in_specs=[
            pl.BlockSpec((1, group * TILE, length, channels), lambda b, i: (b, i, 0, 0)),
            pl.BlockSpec(wide.shape, lambda b, i: (0, 0)),
        ],
        out_specs=pl.BlockSpec((1, group, tall, length), lambda b, i: (b, i, 0, 0)),
        out_shape=jax.ShapeDtypeStruct((chains, blocks, tall, length), F32),
        compiler_params=params(),
        cost_estimate=pl.CostEstimate(flops=2 * pair.size * tall, bytes_accessed=2 * pair.size, transcendentals=0),
        name="pair_bias",
    )(pair, wide)


def attend_kernel(factor, bias_ref, q_ref, k_ref, v_ref, mask_ref, probs_ref, out_ref):
    heads = mask_ref.shape[0] // TILE
    keys, values, mask = k_ref[0], v_ref[0], mask_ref[...]
    for n in range(bias_ref.shape[1]):
        at = pl.ds(n * TILE, TILE)
        wide = jnp.concatenate([q_ref[at, :]] * heads, axis=0) * mask
        scores = dot(wide, keys, NT) * factor + bias_ref[0, n]
        powers = jnp.exp(scores - jnp.max(scores, axis=-1, keepdims=True))
        probs = powers * (1.0 / jnp.sum(powers, axis=-1, keepdims=True))
        probs_ref[0, n] = probs
        mixed = dot(probs.astype(BF16), values) * mask.astype(F32)
        total = mixed[:TILE]
        for h in range(1, heads):
            total = total + mixed[h * TILE : (h + 1) * TILE]
        out_ref[at, :] = total


def attend(bias, queries, keys, values, mask, factor, group=4):
    chains, blocks, tall, length = bias.shape
    width = mask.shape[1]
    rows = chains * blocks * TILE
    steps = blocks // group
    row_spec = pl.BlockSpec((group * TILE, width), lambda b, i: (b * steps + i, 0))
    square = pl.BlockSpec((1, group, tall, length), lambda b, i: (b, i, 0, 0))
    return pl.pallas_call(
        functools.partial(attend_kernel, factor),
        grid=(chains, steps),
        in_specs=[
            square,
            row_spec,
            pl.BlockSpec((1, length, width), lambda b, i: (b, 0, 0)),
            pl.BlockSpec((1, length, width), lambda b, i: (b, 0, 0)),
            pl.BlockSpec(mask.shape, lambda b, i: (0, 0)),
        ],
        out_specs=[square, row_spec],
        out_shape=[jax.ShapeDtypeStruct(bias.shape, F32), jax.ShapeDtypeStruct((rows, width), F32)],
        compiler_params=params(),
        cost_estimate=pl.CostEstimate(flops=4 * bias.size * width, bytes_accessed=10 * bias.size, transcendentals=bias.size),
        name="attend",
    )(bias, queries, keys, values, mask)


def attend_back_kernel(factor, place_ref, probs_ref, q_ref, g_ref, k_ref, v_ref, mask_ref, ds_ref, dq_ref, dk_ref, dv_ref,
                       keep_ref, give_ref, dk_sum, dv_sum):
    heads = mask_ref.shape[0] // TILE
    keys, values, mask = k_ref[0], v_ref[0], mask_ref[...]

    @pl.when(pl.program_id(1) == 0)
    def _():
        dk_sum[...] = jnp.zeros_like(dk_sum)
        dv_sum[...] = jnp.zeros_like(dv_sum)

    for n in range(probs_ref.shape[1]):
        at = pl.ds(n * TILE, TILE)
        probs = probs_ref[0, n]
        queries = jnp.concatenate([q_ref[at, :]] * heads, axis=0) * mask
        grads = jnp.concatenate([g_ref[at, :]] * heads, axis=0) * mask
        probs_grad = dot(grads, values, NT)
        inner = jnp.sum(probs_grad * probs, axis=-1, keepdims=True)
        scores_grad = (probs * (probs_grad - inner)).astype(BF16)
        ds_ref[0, n] = scores_grad
        mixed = dot(scores_grad, keys) * mask.astype(F32)
        total = mixed[:TILE]
        for h in range(1, heads):
            total = total + mixed[h * TILE : (h + 1) * TILE]
        dq_ref[at, :] = (total * factor).astype(BF16)
        dk_sum[...] += dot(scores_grad, queries, TN)
        dv_sum[...] += dot(probs.astype(BF16), grads, TN)

    @pl.when(pl.program_id(1) == pl.num_programs(1) - 1)
    def _():
        dk_ref[0] = (dk_sum[...] * factor).astype(BF16)
        dv_ref[0] = dv_sum[...].astype(BF16)
        local = keep_ref.shape[1]
        for ref, place in ((keep_ref, place_ref[0]), (give_ref, 1 - place_ref[0])):
            at = pl.ds(pl.multiple_of(place * local, local), local)
            ref[0, :, : dk_sum.shape[1]] = (dk_sum[at, :] * factor).astype(BF16)
            ref[0, :, dk_sum.shape[1] :] = dv_sum[at, :].astype(BF16)


def attend_back(place, probs, queries, grads, keys, values, mask, factor, group=4):
    chains, blocks, tall, length = probs.shape
    width = mask.shape[1]
    rows = chains * blocks * TILE
    steps = blocks // group
    row_spec = pl.BlockSpec((group * TILE, width), lambda b, i: (b * steps + i, 0))
    square = pl.BlockSpec((1, group, tall, length), lambda b, i: (b, i, 0, 0))
    return pl.pallas_call(
        functools.partial(attend_back_kernel, factor),
        grid=(chains, steps),
        in_specs=[
            pl.BlockSpec(memory_space=pltpu.SMEM),
            square,
            row_spec,
            row_spec,
            pl.BlockSpec((1, length, width), lambda b, i: (b, 0, 0)),
            pl.BlockSpec((1, length, width), lambda b, i: (b, 0, 0)),
            pl.BlockSpec(mask.shape, lambda b, i: (0, 0)),
        ],
        out_specs=[square, row_spec] + [pl.BlockSpec((1, length, width), lambda b, i: (b, 0, 0))] * 2
        + [pl.BlockSpec((1, blocks * TILE, 2 * width), lambda b, i: (b, 0, 0))] * 2,
        out_shape=[
            jax.ShapeDtypeStruct(probs.shape, BF16),
            jax.ShapeDtypeStruct((rows, width), BF16),
            jax.ShapeDtypeStruct((chains, length, width), BF16),
            jax.ShapeDtypeStruct((chains, length, width), BF16),
            jax.ShapeDtypeStruct((chains, blocks * TILE, 2 * width), BF16),
            jax.ShapeDtypeStruct((chains, blocks * TILE, 2 * width), BF16),
        ],
        scratch_shapes=[pltpu.VMEM((length, width), F32), pltpu.VMEM((length, width), F32)],
        compiler_params=params(),
        cost_estimate=pl.CostEstimate(flops=10 * probs.size * width, bytes_accessed=6 * probs.size, transcendentals=0),
        name="attend_back",
    )(place, probs, queries, grads, keys, values, mask)


def pair_back_kernel(ds_ref, pair_ref, tall_ref, turn_ref, old_dw_ref, *rest):
    grad_ref, dw_ref = rest[-2:]

    @pl.when(pl.program_id(0) == 0)
    def _():
        dw_ref[...] = old_dw_ref[...]

    tall = tall_ref[...]
    total = dw_ref[...]
    for n in range(ds_ref.shape[1]):
        scores_grad = ds_ref[0, n]
        by_row = dot(turn_ref[...], scores_grad).astype(BF16)
        turned = scores_grad.T
        lanes = lax.broadcasted_iota(jnp.int32, turned.shape, 1) % TILE
        for i in range(TILE):
            at = n * TILE + i
            grad_ref[0, at] = dot(jnp.where(lanes == i, turned, jnp.zeros_like(turned)), tall).astype(BF16)
            total = total + dot(by_row[i * TILE : (i + 1) * TILE], pair_ref[0, at])
    dw_ref[...] = total


def pair_back(scores_grad, pair, tall, turn, start, count, old_dw, *old, group=2):
    chains, local, length, channels = pair.shape
    blocks, high = scores_grad.shape[1:3]
    blocks = blocks // group
    place = lambda i: ((start + i) // blocks, (start + i) % blocks, 0, 0)
    size = pair.size * count // (chains * blocks)
    fixed = lambda i: (0, 0)
    return pl.pallas_call(
        pair_back_kernel,
        grid=(count,),
        in_specs=[
            pl.BlockSpec((1, group, high, length), place),
            pl.BlockSpec((1, group * TILE, length, channels), place),
            pl.BlockSpec(tall.shape, fixed),
            pl.BlockSpec(turn.shape, fixed),
            pl.BlockSpec((TILE, channels), fixed),
        ]
        + [pl.BlockSpec(memory_space=pl.ANY)] * len(old),
        out_specs=[
            pl.BlockSpec((1, group * TILE, length, channels), place),
            pl.BlockSpec((TILE, channels), fixed),
        ],
        out_shape=[jax.ShapeDtypeStruct(pair.shape, BF16), jax.ShapeDtypeStruct((TILE, channels), F32)],
        input_output_aliases={5: 0} if old else {},
        compiler_params=params(),
        cost_estimate=pl.CostEstimate(flops=4 * size * high, bytes_accessed=4 * size, transcendentals=0),
        name="pair_back",
    )(scores_grad, pair, tall, turn, old_dw, *old)


def feed_kernel(steps, rows_ref, turned_ref, g_ref, order_ref, line_ref, gate_ref, up_ref, down_ref,
                out_ref, back_ref, *rest):
    grads_refs, held = rest[:-1], rest[-1]
    step = pl.program_id(0)
    per = held.shape[4] // steps
    shape = grads_refs[0].shape

    @pl.when(step == 0)
    def _():
        out_ref[...] = jnp.zeros_like(out_ref)
        back_ref[...] = jnp.zeros_like(back_ref)

    @pl.when(step < steps)
    def _():
        rows, grads = rows_ref[...], g_ref[...]
        w_gate, w_up = gate_ref[...], up_ref[...]
        width = rows.shape[1]
        stack = [down_ref[:, k * width : (k + 1) * width] for k in range(down_ref.shape[1] // width)]
        w_down = dot(line_ref[...], jnp.concatenate(stack, axis=0)).astype(BF16)
        gate = dot(rows, w_gate)
        up = dot(rows, w_up)
        sig = jax.nn.sigmoid(gate)
        silu = gate * sig
        hidden = (silu * up).astype(BF16)
        out_ref[...] += dot(hidden, w_down)
        hidden_grad = dot(grads, w_down, NT)
        gate_grad = (hidden_grad * up * (sig + silu * (1.0 - sig))).astype(BF16)
        up_grad = (hidden_grad * silu).astype(BF16)
        back_ref[...] += dot(gate_grad, w_gate, NT) + dot(up_grad, w_up, NT)
        for k, right in enumerate((gate_grad, up_grad)):
            full = dot(turned_ref[k], right).reshape((2,) + shape).astype(BF16)
            grads_refs[2 * k][...] = full[0]
            grads_refs[2 * k + 1][...] = full[1]
        hidden_turned = dot(order_ref[...], hidden, NT).astype(BF16)
        full = dot(hidden_turned, grads)
        full = full.reshape(held.shape[:4] + (per,) + shape[2:3] + (width,)).astype(BF16)
        held[:, :, :, :, pl.ds(step * per, per)] = full

    for route in range(2):
        for n in range(held.shape[1]):
            @pl.when(step == steps + n)
            def _(route=route, n=n):
                grads_refs[2 * route][...] = held[route, n, 0]
                grads_refs[2 * route + 1][...] = held[route, n, 1]


def feed(rows, turned, grads, order, line, weights, nz):
    count, width = rows.shape
    hidden = weights.shape[1] // 3
    block = order.shape[0]
    steps = hidden // block
    groups = hidden // width
    own = width // (8 * nz)
    fixed = lambda m: (0, 0)
    last = steps - 1
    columns = hidden + groups // 2 * width
    halves = jax.ShapeDtypeStruct((4, nz, own, columns), BF16)
    return pl.pallas_call(
        functools.partial(feed_kernel, steps),
        grid=(steps + groups // 2,),
        in_specs=[
            pl.BlockSpec((count, width), fixed),
            pl.BlockSpec((2, width, count), lambda m: (0, 0, 0)),
            pl.BlockSpec((count, width), fixed),
            pl.BlockSpec((block, block), fixed),
            pl.BlockSpec((block, block), fixed),
            pl.BlockSpec((width, block), lambda m: (0, jnp.minimum(m, last))),
            pl.BlockSpec((width, block), lambda m: (0, steps + jnp.minimum(m, last))),
            pl.BlockSpec((width // steps, hidden), lambda m: (jnp.minimum(m, last), 2)),
        ],
        out_specs=[
            pl.BlockSpec((count, width), fixed),
            pl.BlockSpec((count, width), fixed),
            *[pl.BlockSpec((4, nz, own, block), lambda m: (0, 0, 0, m))] * 4,
        ],
        out_shape=[
            jax.ShapeDtypeStruct((count, width), F32),
            jax.ShapeDtypeStruct((count, width), F32),
            *[halves] * 4,
        ],
        scratch_shapes=[pltpu.VMEM((2, groups // 2, 2, 4, nz, own, width), BF16)],
        compiler_params=params(),
        cost_estimate=pl.CostEstimate(flops=24 * count * width * hidden, bytes_accessed=12 * width * hidden, transcendentals=count * hidden),
        name="feed",
    )(rows, turned, grads, order, line, weights, weights, weights)


def join_kernel(cuts, *refs):
    at = 0
    for which, start, size in cuts:
        piece = refs[which][:, start : start + size] if len(refs[which].shape) == 2 else refs[which][start]
        refs[-1][:, at : at + piece.shape[1]] = piece
        at += piece.shape[1]


def join(arrays, cuts):
    return pl.pallas_call(
        functools.partial(join_kernel, cuts),
        out_shape=jax.ShapeDtypeStruct((arrays[0].shape[0], sum(c[2] for c in cuts)), BF16),
        compiler_params=params(),
        name="join",
    )(*arrays)


def project_kernel(own_ref, all_ref, first_ref, second_ref, q_ref, k_ref, v_ref, gate_ref):
    width = own_ref.shape[1]
    own, every = own_ref[...], all_ref[...]
    q_ref[...] = dot(own, first_ref[:, :width]).astype(BF16)
    k_ref[...] = dot(every, first_ref[:, width : 2 * width]).astype(BF16)
    v_ref[...] = dot(every, second_ref[:, :width]).astype(BF16)
    gate_ref[...] = dot(own, second_ref[:, width : 2 * width])


def project(own, every, first, second):
    count, width = own.shape
    many = every.shape[0]
    return pl.pallas_call(
        project_kernel,
        out_shape=[
            jax.ShapeDtypeStruct((count, width), BF16),
            jax.ShapeDtypeStruct((many, width), BF16),
            jax.ShapeDtypeStruct((many, width), BF16),
            jax.ShapeDtypeStruct((count, width), F32),
        ],
        compiler_params=params(),
        cost_estimate=pl.CostEstimate(flops=4 * (count + many) * width * width, bytes_accessed=12 * width * width, transcendentals=0),
        name="project",
    )(own, every, first, second)


def project_back_kernel(own_ref, all_ref, gated_ref, dq_ref, dk_ref, dv_ref, dg_ref, out_ref, *sums):
    width = own_ref.shape[1]
    half = width // 2
    for k, (inner, outer) in enumerate((((own_ref, dq_ref), (all_ref, dk_ref)), ((all_ref, dv_ref), (own_ref, dg_ref)))):
        for n, rows in enumerate((slice(0, half // 2), slice(half // 2, half), slice(half, width))):
            result = sums[3 * k + n]
            result[:, :width] = dot(inner[0][k, rows], inner[1][...]).astype(BF16)
            result[:, width : 2 * width] = dot(outer[0][k, rows], outer[1][...]).astype(BF16)
            result[:, 2 * width :] = dot(gated_ref[k, rows], out_ref[:, k * half : (k + 1) * half]).astype(BF16)


def project_back(own, every, gated, dq, dk, dv, dg, out):
    width = own.shape[1]
    return pl.pallas_call(
        project_back_kernel,
        out_shape=[jax.ShapeDtypeStruct((width // n, 5 * width // 2), BF16) for n in (4, 4, 2)] * 2,
        compiler_params=params(),
        cost_estimate=pl.CostEstimate(flops=16 * own.size * width, bytes_accessed=16 * width * width, transcendentals=0),
        name="project_back",
    )(own, every, gated, dq, dk, dv, dg, out)


def on_device(sizes, tokens, pair, cath_class, cath_arch, cath_topo, times, out_grad,
              emb_class, emb_arch, emb_topo, w_time, w_ada, w_qkv, w_gate, w_out, w_pair,
              w_ffgate, w_ffup, w_ffdown):
    nz, nx, nc, ny = sizes
    ndp = nz * nx * nc
    devices = ndp * ny
    chains, local, width = tokens.shape
    length = pair.shape[2]
    heads = w_pair.shape[1]
    head = width // heads
    factor = head ** (-0.5)
    rows = chains * local
    own = emb_class.shape[1]
    hidden_width = w_ffgate.shape[1]
    time_rows = w_time.shape[0]

    half = width // 2
    groups = w_ffdown.shape[0] // own
    routes = (("y", "x"), ("x", "y"))
    stacked = join(
        (w_ffgate, w_ffup, w_ffdown.reshape(groups, own, width)),
        [(0, 0, hidden_width), (1, 0, hidden_width)] + [(2, k, width) for k in range(groups)],
    )
    weights = lax.all_gather(stacked, ALL, axis=0, tiled=True)
    packed = join(
        (w_qkv, w_gate, w_out),
        [(0, 0, 2 * width), (2, 0, half), (0, 2 * width, width), (1, 0, width), (2, half, half)],
    )
    attention = Gathering(packed, nz, routes)
    tokens_other = swap(tokens, "y")

    facts = jnp.stack([cath_class.astype(F32), cath_arch.astype(F32), cath_topo.astype(F32), times]).reshape(1, -1)
    pair_rows_w = w_pair.astype(F32).reshape(1, -1)
    pack = jnp.concatenate(
        [
            w_time.astype(F32).reshape(time_rows, devices, own).transpose(1, 0, 2).reshape(devices, -1),
            jnp.broadcast_to(facts, (devices, facts.shape[1])),
            jnp.broadcast_to(pair_rows_w, (devices, pair_rows_w.shape[1])),
        ],
        axis=1,
    )
    got = lax.all_to_all(pack, ALL, split_axis=0, concat_axis=0, tiled=True)
    size_time = time_rows * own
    time_columns = got[:, :size_time].reshape(devices * time_rows, own).astype(BF16)
    size_facts = 4 * chains
    everyone = got[:, size_time : size_time + size_facts].reshape(ndp, ny, 4, chains)[:, 0]
    everyone = everyone.transpose(1, 0, 2).reshape(4, ndp * chains)
    full_pair_w = got[:, size_time + size_facts :].reshape(-1, heads).astype(BF16)
    labels = everyone[:3].astype(jnp.int32)
    features = time_features(everyone[3], devices * time_rows).astype(BF16)
    hot = [
        (labels[k][:, None] == jnp.arange(table.shape[0], dtype=jnp.int32)[None, :]).astype(BF16)
        for k, table in enumerate((emb_class, emb_arch, emb_topo))
    ]
    before = dot(hot[0], emb_class) + dot(hot[1], emb_arch) + dot(hot[2], emb_topo) + dot(features, time_columns)
    sig_before = jax.nn.sigmoid(before)
    condition_low = (before * sig_before).astype(BF16)
    modes_part = dot(condition_low, w_ada)
    modes = lax.all_to_all(modes_part.reshape(ndp, chains, 6 * width), DP, split_axis=0, concat_axis=0, tiled=True)
    modes = jnp.sum(modes, axis=0)
    modes = modes + swap(modes, "y")
    shift_one, scale_one, gate_one, shift_two, scale_two, gate_two = (
        m[:, None, :] for m in jnp.split(modes, 6, axis=-1)
    )

    entry = tokens.astype(F32)
    norm_one, root_one = normalise(entry)
    normed_one = (norm_one * (1.0 + scale_one) + shift_one).astype(BF16)
    norm_other, _ = normalise(tokens_other.astype(F32))
    normed_other = (norm_other * (1.0 + scale_one) + shift_one).astype(BF16)
    normed_all = ordered(normed_one, normed_other, "y", 1).reshape(chains * length, width)
    normed_one = normed_one.reshape(rows, width)
    mask = (jnp.arange(heads * TILE)[:, None] // TILE == jnp.arange(width)[None, :] // head).astype(BF16)
    wide_pair = jnp.repeat(full_pair_w, TILE, axis=1)
    attention.first()
    bias = pair_bias(after(pair, *attention.full), wide_pair)
    attention.got[0] = after(attention.got[0], bias)
    attention.second()
    hots = [spread(own, route, nz) for route in routes]
    steps = hidden_width // width
    order = down_order(own, groups, routes, nz // steps)
    in_turned = jnp.stack([relative(normed_one, hot) for hot in hots])
    all_turned = jnp.stack([relative(normed_all, hot) for hot in hots])
    attention.third()
    first_w, second_w = attention.total()
    full_out = jnp.concatenate([first_w[:, 2 * width :], second_w[:, 2 * width :]], axis=1)
    queries, keys, values, gate_logits = project(normed_one, normed_all, first_w, second_w)
    keys, values = keys.reshape(chains, length, width), values.reshape(chains, length, width)
    sigmoid_gate = jax.nn.sigmoid(gate_logits)
    probs, attended = attend(bias, queries, keys, values, mask, factor)
    gated = (attended * sigmoid_gate).astype(BF16)
    branch_one = dot(gated, full_out).reshape(chains, local, width)
    middle = entry + gate_one * branch_one
    norm_two, root_two = normalise(middle)
    normed_two = (norm_two * (1.0 + scale_two) + shift_two).astype(BF16).reshape(rows, width)
    upstream = out_grad.astype(F32)
    branch_two_grad = (gate_two * upstream).astype(BF16).reshape(rows, width)
    out_turned = jnp.stack([relative(gated, hot) for hot in hots])
    turned = jnp.stack([relative(normed_two, hots[k]) for k in (1, 0)])
    new = jnp.arange(width, dtype=jnp.int32)
    per_step = width // (steps * own)
    old = (new // own % groups) * (per_step * own) + new // (groups * own) * own + new % own
    line = (jnp.arange(width, dtype=jnp.int32)[None, :] == old[:, None]).astype(BF16)
    turn_rows = jnp.arange(TILE * TILE)[:, None]
    turn_columns = jnp.arange(heads * TILE)[None, :]
    turn = ((turn_rows // TILE == turn_columns % TILE) & (turn_rows % TILE == turn_columns // TILE)).astype(BF16)
    tall_pair = wide_pair.T
    weights = after(weights, out_turned, turned, in_turned, all_turned, turn, tall_pair)
    branch_two, normed_two_grad, *grads = feed(normed_two, turned, branch_two_grad, order, line, weights, nz)
    feed_sums = [Reduction(grads[2 * k], grads[2 * k + 1], nz, routes[1 - k]) for k in range(2)]
    split = lambda v: v.reshape(-1, nz, own, v.shape[-1])

    def sum_modes(parts):
        mine = jnp.concatenate(parts, axis=-1)
        return mine, swap(mine, "y")

    def share_modes(mine, other, *needed):
        mine = mine + after(other, *needed)
        mine = jnp.broadcast_to(mine[None], (ndp,) + mine.shape)
        return lax.all_to_all(mine, DP, split_axis=0, concat_axis=0, tiled=True)

    normed_two_grad = normed_two_grad.reshape(chains, local, width)
    middle_grad = upstream + normalise_back(normed_two_grad, scale_two, norm_two, root_two)
    branch_one_grad = (gate_one * middle_grad).astype(BF16).reshape(rows, width)
    gated_grad = dot(branch_one_grad, full_out, NT)
    attended_grad = (gated_grad * sigmoid_gate).astype(BF16)
    logits_grad = (gated_grad * attended * (sigmoid_gate * (1.0 - sigmoid_gate))).astype(BF16)
    branch_two = branch_two.reshape(chains, local, width)
    gate_one_grad = jnp.sum(middle_grad * branch_one, axis=1)
    shift_two_grad = jnp.sum(normed_two_grad, axis=1)
    scale_two_grad = jnp.sum(normed_two_grad * norm_two, axis=1)
    gate_two_grad = jnp.sum(upstream * branch_two, axis=1)
    result = (middle + gate_two * branch_two).astype(BF16)
    for s in feed_sums:
        s.first()
    attended_grad = after(attended_grad, *[s.give for s in feed_sums])
    late_halves = sum_modes([gate_one_grad, shift_two_grad, scale_two_grad, gate_two_grad])
    place = lax.axis_index("y").astype(jnp.int32)
    scores_grad, query_grad, key_grad, value_grad, keep, give = attend_back(
        place.reshape(1), probs, queries, attended_grad, keys, values, mask, factor
    )
    kept_sent = project_back(
        in_turned, all_turned, out_turned, query_grad, key_grad.reshape(-1, width), value_grad.reshape(-1, width),
        logits_grad, branch_one_grad,
    )
    kept_sent = [split(v) for v in kept_sent]
    in_sums = [Reduction(tuple(kept_sent[3 * k : 3 * k + 2]), kept_sent[3 * k + 2], nz, routes[k]) for k in range(2)]
    got = swap(give, "y")
    pair_sums = (jnp.zeros((TILE, pair.shape[3]), F32),)
    steps_all = chains * (local // TILE) // 2
    quarter = steps_all // 4

    def more_pair(start, count, *needed):
        new_grad, new_sum = pair_back(after(scores_grad, *needed), pair, tall_pair, turn, start, count, *pair_sums)
        return (new_sum, new_grad)

    late_modes = share_modes(*late_halves, kept_sent[0])
    pair_sums = more_pair(0, quarter, kept_sent[0])
    for s in feed_sums:
        s.got = after(s.got, pair_sums[0])
        s.second()
    pair_sums = more_pair(quarter, quarter, late_modes, *[s.give for s in feed_sums])
    for s in in_sums:
        s.got = after(s.got, pair_sums[0])
        s.first()
    owned = add_low(keep, after(got, *[s.give for s in in_sums])).reshape(rows, 2 * width)
    normed_one_grad = (
        dot(query_grad, first_w[:, :width], NT)
        + dot(owned[:, :width], first_w[:, width : 2 * width], NT)
        + dot(owned[:, width:], second_w[:, :width], NT)
        + dot(logits_grad, second_w[:, width : 2 * width], NT)
    ).reshape(chains, local, width)
    shift_one_grad = jnp.sum(normed_one_grad, axis=1)
    scale_one_grad = jnp.sum(normed_one_grad * norm_one, axis=1)
    early_halves = sum_modes([shift_one_grad, scale_one_grad])
    for s in feed_sums:
        s.got = after(s.got, normed_one_grad)
    feed_line = Line([s.third() for s in feed_sums], nz)
    early_modes = share_modes(*early_halves, *feed_line.sent)
    pair_sums = more_pair(2 * quarter, steps_all - 2 * quarter, *feed_line.sent, *early_halves)
    tokens_grad = (middle_grad + normalise_back(normed_one_grad, scale_one, norm_one, root_one)).astype(BF16)
    for s in in_sums:
        s.got = after(s.got, pair_sums[0])
        s.second()
    early_modes = after(early_modes, *[s.give for s in in_sums]).reshape(ndp * chains, -1)
    late_modes = late_modes.reshape(ndp * chains, -1)
    pair_w_sum, pair_grad = pair_sums
    grad_pair_w = pair_w_sum[:heads].T

    low_f32, ada_f32 = condition_low.astype(F32), w_ada.astype(F32)
    exact = lambda left, right, dims: lax.dot_general(left, right, (dims, ((), ())), precision=HIGH)
    cut = 2 * width
    grad_ada = jnp.concatenate([exact(low_f32, early_modes, TN), exact(low_f32, late_modes, TN)], axis=1)
    condition_grad = exact(early_modes, ada_f32[:, :cut], NT) + exact(late_modes, ada_f32[:, cut:], NT)
    before_grad = condition_grad * (sig_before * (1.0 + before * (1.0 - sig_before)))
    outer = lambda left: lax.dot_general(left.astype(F32), before_grad, (((0,), (0,)), ((), ())), precision=HIGH)
    grad_class, grad_arch, grad_topo = outer(hot[0]), outer(hot[1]), outer(hot[2])
    time_pack = jnp.concatenate(
        [outer(features).reshape(devices, time_rows * own), grad_pair_w.reshape(devices, -1)], axis=1
    )
    time_got = lax.all_to_all(time_pack, ALL, split_axis=0, concat_axis=0, tiled=True)
    for r in in_sums:
        r.got = after(r.got, time_pack)
    in_line = Line([r.third() for r in in_sums], nz)
    feed_total = feed_line.total(time_pack, *in_line.sent)
    early, late = jnp.split(feed_total, 2, axis=1)
    sum_gate, sum_up = early[:, :hidden_width], late[:, :hidden_width]
    sum_down = jnp.concatenate(
        [t[:, hidden_width + k * width : hidden_width + (k + 1) * width] for t in (early, late) for k in range(groups // 2)], axis=0
    )
    sums = jnp.split(in_line.total(), 2, axis=1)
    sum_out = jnp.concatenate([s[:, 2 * width :] for s in sums], axis=1)
    grad_time = time_got[:, :size_time].reshape(devices, time_rows, own).transpose(1, 0, 2).reshape(time_rows, width)
    grad_pair_own = jnp.sum(time_got[:, size_time:], axis=0).reshape(w_pair.shape)

    return (
        result,
        tokens_grad,
        pair_grad,
        grad_class,
        grad_arch,
        grad_topo,
        grad_time,
        grad_ada,
        jnp.concatenate([sums[0][:, : 2 * width], sums[1][:, :width]], axis=1),
        sums[1][:, width : 2 * width],
        sum_out,
        grad_pair_own,
        sum_gate,
        sum_up,
        sum_down,
    )


def solution(mesh):
    ndp, ny = mesh.shape["dp"], mesh.shape["seq"]
    sizes = (ndp // 4, 2, 2, ny)
    fine = Mesh(mesh.devices.reshape(sizes), ALL)
    row, col = P(ALL, None), P(None, ALL)
    in_specs = (P(DP, "y", None), P(DP, "y", None, None), P(DP), P(DP), P(DP), P(DP), P(DP, "y", None)) + (col,) * 3 + (row,) * 9
    out_specs = (P(DP, "y", None), P(DP, "y", None), P(DP, "y", None, None)) + (col,) * 3 + (row,) * 9

    def body(*args):
        return on_device(sizes, *args)

    return jax.shard_map(body, mesh=fine, in_specs=in_specs, out_specs=out_specs, check_vma=False)
```

```python
import functools
import math

import jax
import jax.numpy as jnp
from jax import lax
from jax.experimental import pallas as pl
from jax.experimental.pallas import tpu as pltpu
from jax.sharding import Mesh
from jax.sharding import PartitionSpec as P

EPSILON = 1e-06
TIME_SCALE = 100.0
F32 = jnp.float32
BF16 = jnp.bfloat16
DP = ("z", "x", "c")
ALL = ("z", "x", "c", "y")
HIGH = lax.Precision.HIGHEST
NT, TN = ((1,), (1,)), ((0,), (0,))
TILE = 16
VMEM = 60 * 1024 * 1024


def dot(left, right, dims=((1,), (0,))):
    return lax.dot_general(left, right, (dims, ((), ())), preferred_element_type=F32)


def params():
    return pltpu.CompilerParams(vmem_limit_bytes=VMEM)


def time_features(moment, width):
    half_width = width // 2
    frequency = jnp.exp(-math.log(10000.0) * jnp.arange(half_width, dtype=F32) / half_width)
    angles = TIME_SCALE * moment[:, None] * frequency[None, :]
    return jnp.concatenate([jnp.sin(angles), jnp.cos(angles)], axis=-1)


def normalise(rows):
    centre = rows - jnp.mean(rows, axis=-1, keepdims=True)
    spread = jnp.mean(centre * centre, axis=-1, keepdims=True)
    root = lax.rsqrt(spread + EPSILON)
    return centre * root, root


def normalise_back(grad, scale, normed, root):
    u = grad * (1.0 + scale)
    inner = u - jnp.mean(u, axis=-1, keepdims=True)
    return root * (inner - normed * jnp.mean(u * normed, axis=-1, keepdims=True))


def swap(value, axis):
    return lax.ppermute(value, axis, [(0, 1), (1, 0)])


def shift(value, axis, size, by):
    return lax.ppermute(value, axis, [(i, (i + by) % size) for i in range(size)])


def add_low(left, right):
    return (left.astype(F32) + right.astype(F32)).astype(BF16)


def after(value, *others):
    return lax.optimization_barrier((value, *others))[0]


def ordered(own, other, axis, at):
    low = jnp.stack([own, other], axis=at)
    high = jnp.stack([other, own], axis=at)
    return jnp.where(lax.axis_index(axis) == 0, low, high)


class Gathering:
    def __init__(self, block, nz, routes):
        self.nz, self.routes, self.block = nz, routes, block
        self.got = [shift(block, "z", nz, by) for by in range(1, nz)]

    def first(self):
        nz = self.nz
        parts = [self.block] + self.got
        line = jnp.stack([parts[(nz - 1 - i) % nz] for i in range(2 * nz - 1)])
        full = lax.dynamic_slice_in_dim(line, nz - 1 - lax.axis_index("z"), nz, 0)
        half = full.shape[-1] // 2
        self.full = [full[..., :half], full[..., half:]]
        self.got = [swap(f, r[0]) for f, r in zip(self.full, self.routes)]

    def second(self):
        self.full = [ordered(f, g, r[0], 1) for f, g, r in zip(self.full, self.got, self.routes)]
        self.got = [swap(f, r[1]) for f, r in zip(self.full, self.routes)]

    def third(self):
        self.full = [ordered(f, g, r[1], 2 if r[1] == "y" else 1) for f, g, r in zip(self.full, self.got, self.routes)]
        self.got = [swap(f, "c") for f in self.full]

    def total(self):
        return [ordered(f, g, "c", 2).reshape(-1, f.shape[-1]) for f, g in zip(self.full, self.got)]


def spread(rows, order, nz):
    n = 8 * nz * rows
    new = jnp.arange(n, dtype=jnp.int32)
    part = new // (nz * rows)
    at = {"c": part // 4, order[0]: part // 2 % 2, order[1]: part % 2}
    at = {k: v ^ lax.axis_index(k) for k, v in at.items()}
    old = (((new // rows % nz * 2 + at["x"]) * 2 + at["c"]) * 2 + at["y"]) * rows + new % rows
    return (jnp.arange(n, dtype=jnp.int32)[:, None] == old[None, :]).astype(BF16)


def down_order(rows, groups, routes, nz):
    n = 8 * nz * rows * groups
    new = jnp.arange(n, dtype=jnp.int32)
    group = new // (8 * nz * rows)
    part = new // (nz * rows) % 8
    late = group >= groups // 2
    firsts, seconds = part // 2 % 2, part % 2
    at = {"c": part // 4}
    for axis in ("x", "y"):
        early_bit = firsts if routes[1][0] == axis else seconds
        late_bit = firsts if routes[0][0] == axis else seconds
        at[axis] = jnp.where(late, late_bit, early_bit)
    at = {k: v ^ lax.axis_index(k) for k, v in at.items()}
    old = (((new // rows % nz * 2 + at["x"]) * 2 + at["c"]) * 2 + at["y"]) * groups * rows + group * rows + new % rows
    return (jnp.arange(n, dtype=jnp.int32)[None, :] == old[:, None]).astype(BF16)


def relative(value, hot):
    return dot(hot, value, ((0,), (1,))).astype(BF16)


class Reduction:
    def __init__(self, keep, send, nz, order):
        self.keep = keep if isinstance(keep, tuple) else (keep[:2], keep[2:])
        self.nz, self.order = nz, order
        self.got = swap(send, "c")

    def first(self):
        self.give = add_low(self.keep[1], self.got[2:])
        self.keep = add_low(self.keep[0], self.got[:2])
        self.got = swap(self.give, self.order[0])
        return self

    def second(self):
        self.give = add_low(self.keep[1], self.got[1])
        self.keep = add_low(self.keep[0], self.got[0])
        self.got = swap(self.give, self.order[1])
        return self

    def third(self):
        return add_low(self.keep, self.got)


class Line:
    def __init__(self, blocks, nz):
        block = jnp.concatenate(blocks, axis=-1)
        place = lax.axis_index("z")
        self.nz, self.by = nz, 1
        pick = lambda m: lax.dynamic_index_in_dim(block, place ^ m, 0, keepdims=False)
        self.keep = jnp.stack([pick(m) for m in range(0, nz, 2)])
        self.send(jnp.stack([pick(m) for m in range(1, nz, 2)]))

    def send(self, sent):
        self.sent = sent
        self.got = lax.ppermute(sent, "z", [(i, i ^ self.by) for i in range(self.nz)])

    def next(self):
        while self.by * 2 < self.nz:
            self.by *= 2
            total = add_low(self.keep, self.got)
            self.keep = total[::2]
            self.send(total[1::2])

    def total(self, *needed):
        got = after(self.got, *needed)
        return (self.keep.astype(F32) + got.astype(F32))[0]


def bias_kernel(pair_ref, wide_ref, out_ref):
    wide = wide_ref[...]
    lanes = lax.broadcasted_iota(jnp.int32, (pair_ref.shape[2], wide.shape[1]), 1) % TILE
    for n in range(out_ref.shape[1]):
        total = dot(pair_ref[0, n * TILE], wide)
        for i in range(1, TILE):
            total = jnp.where(lanes == i, dot(pair_ref[0, n * TILE + i], wide), total)
        out_ref[0, n] = total.T


def pair_bias(pair, wide, group=4):
    chains, local, length, channels = pair.shape
    blocks, tall = local // TILE, wide.shape[1]
    return pl.pallas_call(
        bias_kernel,
        grid=(chains, blocks // group),
        in_specs=[
            pl.BlockSpec((1, group * TILE, length, channels), lambda b, i: (b, i, 0, 0)),
            pl.BlockSpec(wide.shape, lambda b, i: (0, 0)),
        ],
        out_specs=pl.BlockSpec((1, group, tall, length), lambda b, i: (b, i, 0, 0)),
        out_shape=jax.ShapeDtypeStruct((chains, blocks, tall, length), F32),
        compiler_params=params(),
        cost_estimate=pl.CostEstimate(flops=2 * pair.size * tall, bytes_accessed=2 * pair.size, transcendentals=0),
        name="pair_bias",
    )(pair, wide)


def widen(ref, mask):
    heads, tiles = mask.shape[0] // TILE, ref.shape[0] // TILE
    return jnp.concatenate(
        [jnp.concatenate([ref[n * TILE : (n + 1) * TILE, :]] * heads, axis=0) * mask for n in range(tiles)], axis=0
    )


def narrow(mixed, mask):
    tall = mask.shape[0]
    mask = mask.astype(F32)
    rows = []
    for n in range(mixed.shape[0] // tall):
        own = mixed[n * tall : (n + 1) * tall] * mask
        total = own[:TILE]
        for h in range(1, tall // TILE):
            total = total + own[h * TILE : (h + 1) * TILE]
        rows.append(total)
    return jnp.concatenate(rows, axis=0)


def attend_kernel(factor, bias_ref, q_ref, k_ref, v_ref, mask_ref, probs_ref, out_ref):
    mask = mask_ref[...]
    shape = bias_ref.shape[1:]
    bias = bias_ref[0].reshape(-1, shape[-1])
    scores = dot(widen(q_ref, mask), k_ref[0], NT) * factor + bias
    powers = jnp.exp(scores - jnp.max(scores, axis=-1, keepdims=True))
    probs = powers * (1.0 / jnp.sum(powers, axis=-1, keepdims=True))
    probs_ref[0] = probs.reshape(shape)
    out_ref[...] = narrow(dot(probs.astype(BF16), v_ref[0]), mask)


def attend(bias, queries, keys, values, mask, factor, group=4):
    chains, blocks, tall, length = bias.shape
    width = mask.shape[1]
    rows = chains * blocks * TILE
    steps = blocks // group
    row_spec = pl.BlockSpec((group * TILE, width), lambda b, i: (b * steps + i, 0))
    square = pl.BlockSpec((1, group, tall, length), lambda b, i: (b, i, 0, 0))
    return pl.pallas_call(
        functools.partial(attend_kernel, factor),
        grid=(chains, steps),
        in_specs=[
            square,
            row_spec,
            pl.BlockSpec((1, length, width), lambda b, i: (b, 0, 0)),
            pl.BlockSpec((1, length, width), lambda b, i: (b, 0, 0)),
            pl.BlockSpec(mask.shape, lambda b, i: (0, 0)),
        ],
        out_specs=[square, row_spec],
        out_shape=[jax.ShapeDtypeStruct(bias.shape, F32), jax.ShapeDtypeStruct((rows, width), F32)],
        compiler_params=params(),
        cost_estimate=pl.CostEstimate(flops=4 * bias.size * width, bytes_accessed=10 * bias.size, transcendentals=bias.size),
        name="attend",
    )(bias, queries, keys, values, mask)


def attend_back_kernel(factor, place_ref, probs_ref, q_ref, g_ref, k_ref, v_ref, mask_ref, ds_ref, dq_ref, dk_ref, dv_ref,
                       keep_ref, give_ref, dk_sum, dv_sum):
    keys, values, mask = k_ref[0], v_ref[0], mask_ref[...]

    @pl.when(pl.program_id(1) == 0)
    def _():
        dk_sum[...] = jnp.zeros_like(dk_sum)
        dv_sum[...] = jnp.zeros_like(dv_sum)

    shape = probs_ref.shape[1:]
    probs = probs_ref[0].reshape(-1, shape[-1])
    queries, grads = widen(q_ref, mask), widen(g_ref, mask)
    probs_grad = dot(grads, values, NT)
    inner = jnp.sum(probs_grad * probs, axis=-1, keepdims=True)
    scores_grad = (probs * (probs_grad - inner)).astype(BF16)
    ds_ref[0] = scores_grad.reshape(shape)
    dq_ref[...] = (narrow(dot(scores_grad, keys), mask) * factor).astype(BF16)
    dk_sum[...] += dot(scores_grad, queries, TN)
    dv_sum[...] += dot(probs.astype(BF16), grads, TN)

    @pl.when(pl.program_id(1) == pl.num_programs(1) - 1)
    def _():
        dk_ref[0] = (dk_sum[...] * factor).astype(BF16)
        dv_ref[0] = dv_sum[...].astype(BF16)
        local = keep_ref.shape[1]
        for ref, place in ((keep_ref, place_ref[0]), (give_ref, 1 - place_ref[0])):
            at = pl.ds(pl.multiple_of(place * local, local), local)
            ref[0, :, : dk_sum.shape[1]] = (dk_sum[at, :] * factor).astype(BF16)
            ref[0, :, dk_sum.shape[1] :] = dv_sum[at, :].astype(BF16)


def attend_back(place, probs, queries, grads, keys, values, mask, factor, group=4):
    chains, blocks, tall, length = probs.shape
    width = mask.shape[1]
    rows = chains * blocks * TILE
    steps = blocks // group
    row_spec = pl.BlockSpec((group * TILE, width), lambda b, i: (b * steps + i, 0))
    square = pl.BlockSpec((1, group, tall, length), lambda b, i: (b, i, 0, 0))
    return pl.pallas_call(
        functools.partial(attend_back_kernel, factor),
        grid=(chains, steps),
        in_specs=[
            pl.BlockSpec(memory_space=pltpu.SMEM),
            square,
            row_spec,
            row_spec,
            pl.BlockSpec((1, length, width), lambda b, i: (b, 0, 0)),
            pl.BlockSpec((1, length, width), lambda b, i: (b, 0, 0)),
            pl.BlockSpec(mask.shape, lambda b, i: (0, 0)),
        ],
        out_specs=[square, row_spec] + [pl.BlockSpec((1, length, width), lambda b, i: (b, 0, 0))] * 2
        + [pl.BlockSpec((1, blocks * TILE, 2 * width), lambda b, i: (b, 0, 0))] * 2,
        out_shape=[
            jax.ShapeDtypeStruct(probs.shape, BF16),
            jax.ShapeDtypeStruct((rows, width), BF16),
            jax.ShapeDtypeStruct((chains, length, width), BF16),
            jax.ShapeDtypeStruct((chains, length, width), BF16),
            jax.ShapeDtypeStruct((chains, blocks * TILE, 2 * width), BF16),
            jax.ShapeDtypeStruct((chains, blocks * TILE, 2 * width), BF16),
        ],
        scratch_shapes=[pltpu.VMEM((length, width), F32), pltpu.VMEM((length, width), F32)],
        compiler_params=params(),
        cost_estimate=pl.CostEstimate(flops=10 * probs.size * width, bytes_accessed=6 * probs.size, transcendentals=0),
        name="attend_back",
    )(place, probs, queries, grads, keys, values, mask)


def pair_back_kernel(ds_ref, pair_ref, tall_ref, turn_ref, old_dw_ref, *rest):
    grad_ref, dw_ref = rest[-2:]

    @pl.when(pl.program_id(0) == 0)
    def _():
        dw_ref[...] = old_dw_ref[...]

    tall = tall_ref[...]
    total = dw_ref[...]
    for n in range(ds_ref.shape[1]):
        scores_grad = ds_ref[0, n]
        by_row = dot(turn_ref[...], scores_grad).astype(BF16)
        turned = scores_grad.T
        lanes = lax.broadcasted_iota(jnp.int32, turned.shape, 1) % TILE
        for i in range(TILE):
            at = n * TILE + i
            grad_ref[0, at] = dot(jnp.where(lanes == i, turned, jnp.zeros_like(turned)), tall).astype(BF16)
            total = total + dot(by_row[i * TILE : (i + 1) * TILE], pair_ref[0, at])
    dw_ref[...] = total


def pair_back(scores_grad, pair, tall, turn, start, count, old_dw, *old, group=2):
    chains, local, length, channels = pair.shape
    blocks, high = scores_grad.shape[1:3]
    blocks = blocks // group
    place = lambda i: ((start + i) // blocks, (start + i) % blocks, 0, 0)
    size = pair.size * count // (chains * blocks)
    fixed = lambda i: (0, 0)
    return pl.pallas_call(
        pair_back_kernel,
        grid=(count,),
        in_specs=[
            pl.BlockSpec((1, group, high, length), place),
            pl.BlockSpec((1, group * TILE, length, channels), place),
            pl.BlockSpec(tall.shape, fixed),
            pl.BlockSpec(turn.shape, fixed),
            pl.BlockSpec((TILE, channels), fixed),
        ]
        + [pl.BlockSpec(memory_space=pl.ANY)] * len(old),
        out_specs=[
            pl.BlockSpec((1, group * TILE, length, channels), place),
            pl.BlockSpec((TILE, channels), fixed),
        ],
        out_shape=[jax.ShapeDtypeStruct(pair.shape, BF16), jax.ShapeDtypeStruct((TILE, channels), F32)],
        input_output_aliases={5: 0} if old else {},
        compiler_params=params(),
        cost_estimate=pl.CostEstimate(flops=4 * size * high, bytes_accessed=4 * size, transcendentals=0),
        name="pair_back",
    )(scores_grad, pair, tall, turn, old_dw, *old)


def feed_kernel(steps, rows_ref, turned_ref, g_ref, order_ref, line_ref, gate_ref, up_ref, down_ref,
                out_ref, back_ref, *rest):
    grads_refs, held = rest[:-1], rest[-1]
    step = pl.program_id(0)
    per = held.shape[4] // steps
    shape = grads_refs[0].shape

    @pl.when(step == 0)
    def _():
        out_ref[...] = jnp.zeros_like(out_ref)
        back_ref[...] = jnp.zeros_like(back_ref)

    @pl.when(step < steps)
    def _():
        rows, grads = rows_ref[...], g_ref[...]
        w_gate, w_up = gate_ref[...], up_ref[...]
        width = rows.shape[1]
        stack = [down_ref[:, k * width : (k + 1) * width] for k in range(down_ref.shape[1] // width)]
        w_down = dot(line_ref[...], jnp.concatenate(stack, axis=0)).astype(BF16)
        gate = dot(rows, w_gate)
        up = dot(rows, w_up)
        sig = jax.nn.sigmoid(gate)
        silu = gate * sig
        hidden = (silu * up).astype(BF16)
        out_ref[...] += dot(hidden, w_down)
        hidden_grad = dot(grads, w_down, NT)
        gate_grad = (hidden_grad * up * (sig + silu * (1.0 - sig))).astype(BF16)
        up_grad = (hidden_grad * silu).astype(BF16)
        back_ref[...] += dot(gate_grad, w_gate, NT) + dot(up_grad, w_up, NT)
        for k, right in enumerate((gate_grad, up_grad)):
            full = dot(turned_ref[k], right).reshape((2,) + shape).astype(BF16)
            grads_refs[2 * k][...] = full[0]
            grads_refs[2 * k + 1][...] = full[1]
        hidden_turned = dot(order_ref[...], hidden, NT).astype(BF16)
        full = dot(hidden_turned, grads)
        full = full.reshape(held.shape[:4] + (per,) + shape[2:3] + (width,)).astype(BF16)
        held[:, :, :, :, pl.ds(step * per, per)] = full

    for route in range(2):
        for n in range(held.shape[1]):
            @pl.when(step == steps + n)
            def _(route=route, n=n):
                grads_refs[2 * route][...] = held[route, n, 0]
                grads_refs[2 * route + 1][...] = held[route, n, 1]


def feed(rows, turned, grads, order, line, weights, nz):
    count, width = rows.shape
    hidden = weights.shape[1] // 3
    block = order.shape[0]
    steps = hidden // block
    groups = hidden // width
    own = width // (8 * nz)
    fixed = lambda m: (0, 0)
    last = steps - 1
    columns = hidden + groups // 2 * width
    halves = jax.ShapeDtypeStruct((4, nz, own, columns), BF16)
    return pl.pallas_call(
        functools.partial(feed_kernel, steps),
        grid=(steps + groups // 2,),
        in_specs=[
            pl.BlockSpec((count, width), fixed),
            pl.BlockSpec((2, width, count), lambda m: (0, 0, 0)),
            pl.BlockSpec((count, width), fixed),
            pl.BlockSpec((block, block), fixed),
            pl.BlockSpec((block, block), fixed),
            pl.BlockSpec((width, block), lambda m: (0, jnp.minimum(m, last))),
            pl.BlockSpec((width, block), lambda m: (0, steps + jnp.minimum(m, last))),
            pl.BlockSpec((width // steps, hidden), lambda m: (jnp.minimum(m, last), 2)),
        ],
        out_specs=[
            pl.BlockSpec((count, width), fixed),
            pl.BlockSpec((count, width), fixed),
            *[pl.BlockSpec((4, nz, own, block), lambda m: (0, 0, 0, m))] * 4,
        ],
        out_shape=[
            jax.ShapeDtypeStruct((count, width), F32),
            jax.ShapeDtypeStruct((count, width), F32),
            *[halves] * 4,
        ],
        scratch_shapes=[pltpu.VMEM((2, groups // 2, 2, 4, nz, own, width), BF16)],
        compiler_params=params(),
        cost_estimate=pl.CostEstimate(flops=24 * count * width * hidden, bytes_accessed=12 * width * hidden, transcendentals=count * hidden),
        name="feed",
    )(rows, turned, grads, order, line, weights, weights, weights)


def join_kernel(cuts, *refs):
    at = 0
    for which, start, size in cuts:
        piece = refs[which][:, start : start + size] if len(refs[which].shape) == 2 else refs[which][start]
        refs[-1][:, at : at + piece.shape[1]] = piece
        at += piece.shape[1]


def join(arrays, cuts):
    return pl.pallas_call(
        functools.partial(join_kernel, cuts),
        out_shape=jax.ShapeDtypeStruct((arrays[0].shape[0], sum(c[2] for c in cuts)), BF16),
        compiler_params=params(),
        name="join",
    )(*arrays)


def project_kernel(own_ref, all_ref, first_ref, second_ref, q_ref, k_ref, v_ref, gate_ref):
    width = own_ref.shape[1]
    own, every = own_ref[...], all_ref[...]
    q_ref[...] = dot(own, first_ref[:, :width]).astype(BF16)
    k_ref[...] = dot(every, first_ref[:, width : 2 * width]).astype(BF16)
    v_ref[...] = dot(every, second_ref[:, :width]).astype(BF16)
    gate_ref[...] = dot(own, second_ref[:, width : 2 * width])


def project(own, every, first, second):
    count, width = own.shape
    many = every.shape[0]
    return pl.pallas_call(
        project_kernel,
        out_shape=[
            jax.ShapeDtypeStruct((count, width), BF16),
            jax.ShapeDtypeStruct((many, width), BF16),
            jax.ShapeDtypeStruct((many, width), BF16),
            jax.ShapeDtypeStruct((count, width), F32),
        ],
        compiler_params=params(),
        cost_estimate=pl.CostEstimate(flops=4 * (count + many) * width * width, bytes_accessed=12 * width * width, transcendentals=0),
        name="project",
    )(own, every, first, second)


def project_back_kernel(own_ref, all_ref, gated_ref, dq_ref, dk_ref, dv_ref, dg_ref, out_ref, *sums):
    width = own_ref.shape[1]
    half = width // 2
    for k, (inner, outer) in enumerate((((own_ref, dq_ref), (all_ref, dk_ref)), ((all_ref, dv_ref), (own_ref, dg_ref)))):
        for n, rows in enumerate((slice(0, half // 2), slice(half // 2, half), slice(half, width))):
            result = sums[3 * k + n]
            result[:, :width] = dot(inner[0][k, rows], inner[1][...]).astype(BF16)
            result[:, width : 2 * width] = dot(outer[0][k, rows], outer[1][...]).astype(BF16)
            result[:, 2 * width :] = dot(gated_ref[k, rows], out_ref[:, k * half : (k + 1) * half]).astype(BF16)


def project_back(own, every, gated, dq, dk, dv, dg, out):
    width = own.shape[1]
    return pl.pallas_call(
        project_back_kernel,
        out_shape=[jax.ShapeDtypeStruct((width // n, 5 * width // 2), BF16) for n in (4, 4, 2)] * 2,
        compiler_params=params(),
        cost_estimate=pl.CostEstimate(flops=16 * own.size * width, bytes_accessed=16 * width * width, transcendentals=0),
        name="project_back",
    )(own, every, gated, dq, dk, dv, dg, out)


def on_device(sizes, tokens, pair, cath_class, cath_arch, cath_topo, times, out_grad,
              emb_class, emb_arch, emb_topo, w_time, w_ada, w_qkv, w_gate, w_out, w_pair,
              w_ffgate, w_ffup, w_ffdown):
    nz, nx, nc, ny = sizes
    ndp = nz * nx * nc
    devices = ndp * ny
    chains, local, width = tokens.shape
    length = pair.shape[2]
    heads = w_pair.shape[1]
    head = width // heads
    factor = head ** (-0.5)
    rows = chains * local
    own = emb_class.shape[1]
    hidden_width = w_ffgate.shape[1]
    time_rows = w_time.shape[0]

    half = width // 2
    groups = w_ffdown.shape[0] // own
    routes = (("y", "x"), ("x", "y"))
    stacked = join(
        (w_ffgate, w_ffup, w_ffdown.reshape(groups, own, width)),
        [(0, 0, hidden_width), (1, 0, hidden_width)] + [(2, k, width) for k in range(groups)],
    )
    weights = lax.all_gather(stacked, ALL, axis=0, tiled=True)
    packed = join(
        (w_qkv, w_gate, w_out),
        [(0, 0, 2 * width), (2, 0, half), (0, 2 * width, width), (1, 0, width), (2, half, half)],
    )
    attention = Gathering(packed, nz, routes)
    tokens_other = swap(tokens, "y")

    facts = jnp.stack([cath_class.astype(F32), cath_arch.astype(F32), cath_topo.astype(F32), times]).reshape(1, -1)
    pair_rows_w = w_pair.astype(F32).reshape(1, -1)
    pack = jnp.concatenate(
        [
            w_time.astype(F32).reshape(time_rows, devices, own).transpose(1, 0, 2).reshape(devices, -1),
            jnp.broadcast_to(facts, (devices, facts.shape[1])),
            jnp.broadcast_to(pair_rows_w, (devices, pair_rows_w.shape[1])),
        ],
        axis=1,
    )
    got = lax.all_to_all(pack, ALL, split_axis=0, concat_axis=0, tiled=True)
    size_time = time_rows * own
    time_columns = got[:, :size_time].reshape(devices * time_rows, own).astype(BF16)
    size_facts = 4 * chains
    everyone = got[:, size_time : size_time + size_facts].reshape(ndp, ny, 4, chains)[:, 0]
    everyone = everyone.transpose(1, 0, 2).reshape(4, ndp * chains)
    full_pair_w = got[:, size_time + size_facts :].reshape(-1, heads).astype(BF16)
    labels = everyone[:3].astype(jnp.int32)
    features = time_features(everyone[3], devices * time_rows).astype(BF16)
    hot = [
        (labels[k][:, None] == jnp.arange(table.shape[0], dtype=jnp.int32)[None, :]).astype(BF16)
        for k, table in enumerate((emb_class, emb_arch, emb_topo))
    ]
    before = dot(hot[0], emb_class) + dot(hot[1], emb_arch) + dot(hot[2], emb_topo) + dot(features, time_columns)
    sig_before = jax.nn.sigmoid(before)
    condition_low = (before * sig_before).astype(BF16)
    modes_part = dot(condition_low, w_ada)
    modes = lax.all_to_all(modes_part.reshape(ndp, chains, 6 * width), DP, split_axis=0, concat_axis=0, tiled=True)
    modes = jnp.sum(modes, axis=0)
    modes = modes + swap(modes, "y")
    shift_one, scale_one, gate_one, shift_two, scale_two, gate_two = (
        m[:, None, :] for m in jnp.split(modes, 6, axis=-1)
    )

    entry = tokens.astype(F32)
    norm_one, root_one = normalise(entry)
    normed_one = (norm_one * (1.0 + scale_one) + shift_one).astype(BF16)
    norm_other, _ = normalise(tokens_other.astype(F32))
    normed_other = (norm_other * (1.0 + scale_one) + shift_one).astype(BF16)
    normed_all = ordered(normed_one, normed_other, "y", 1).reshape(chains * length, width)
    normed_one = normed_one.reshape(rows, width)
    mask = (jnp.arange(heads * TILE)[:, None] // TILE == jnp.arange(width)[None, :] // head).astype(BF16)
    wide_pair = jnp.repeat(full_pair_w, TILE, axis=1)
    attention.first()
    bias = pair_bias(after(pair, *attention.full), wide_pair)
    attention.got[0] = after(attention.got[0], bias)
    attention.second()
    hots = [spread(own, route, nz) for route in routes]
    steps = hidden_width // width
    order = down_order(own, groups, routes, nz // steps)
    in_turned = jnp.stack([relative(normed_one, hot) for hot in hots])
    all_turned = jnp.stack([relative(normed_all, hot) for hot in hots])
    attention.third()
    first_w, second_w = attention.total()
    full_out = jnp.concatenate([first_w[:, 2 * width :], second_w[:, 2 * width :]], axis=1)
    queries, keys, values, gate_logits = project(normed_one, normed_all, first_w, second_w)
    keys, values = keys.reshape(chains, length, width), values.reshape(chains, length, width)
    sigmoid_gate = jax.nn.sigmoid(gate_logits)
    probs, attended = attend(bias, queries, keys, values, mask, factor)
    gated = (attended * sigmoid_gate).astype(BF16)
    branch_one = dot(gated, full_out).reshape(chains, local, width)
    middle = entry + gate_one * branch_one
    norm_two, root_two = normalise(middle)
    normed_two = (norm_two * (1.0 + scale_two) + shift_two).astype(BF16).reshape(rows, width)
    upstream = out_grad.astype(F32)
    branch_two_grad = (gate_two * upstream).astype(BF16).reshape(rows, width)
    out_turned = jnp.stack([relative(gated, hot) for hot in hots])
    turned = jnp.stack([relative(normed_two, hots[k]) for k in (1, 0)])
    new = jnp.arange(width, dtype=jnp.int32)
    per_step = width // (steps * own)
    old = (new // own % groups) * (per_step * own) + new // (groups * own) * own + new % own
    line = (jnp.arange(width, dtype=jnp.int32)[None, :] == old[:, None]).astype(BF16)
    turn_rows = jnp.arange(TILE * TILE)[:, None]
    turn_columns = jnp.arange(heads * TILE)[None, :]
    turn = ((turn_rows // TILE == turn_columns % TILE) & (turn_rows % TILE == turn_columns // TILE)).astype(BF16)
    tall_pair = wide_pair.T
    weights = after(weights, out_turned, turned, in_turned, all_turned, turn, tall_pair)
    branch_two, normed_two_grad, *grads = feed(normed_two, turned, branch_two_grad, order, line, weights, nz)
    feed_sums = [Reduction(grads[2 * k], grads[2 * k + 1], nz, routes[1 - k]) for k in range(2)]
    split = lambda v: v.reshape(-1, nz, own, v.shape[-1])

    def sum_modes(parts):
        mine = jnp.concatenate(parts, axis=-1)
        return mine, swap(mine, "y")

    def share_modes(mine, other, *needed):
        mine = mine + after(other, *needed)
        mine = jnp.broadcast_to(mine[None], (ndp,) + mine.shape)
        return lax.all_to_all(mine, DP, split_axis=0, concat_axis=0, tiled=True)

    normed_two_grad = normed_two_grad.reshape(chains, local, width)
    middle_grad = upstream + normalise_back(normed_two_grad, scale_two, norm_two, root_two)
    branch_one_grad = (gate_one * middle_grad).astype(BF16).reshape(rows, width)
    gated_grad = dot(branch_one_grad, full_out, NT)
    attended_grad = (gated_grad * sigmoid_gate).astype(BF16)
    logits_grad = (gated_grad * attended * (sigmoid_gate * (1.0 - sigmoid_gate))).astype(BF16)
    branch_two = branch_two.reshape(chains, local, width)
    gate_one_grad = jnp.sum(middle_grad * branch_one, axis=1)
    shift_two_grad = jnp.sum(normed_two_grad, axis=1)
    scale_two_grad = jnp.sum(normed_two_grad * norm_two, axis=1)
    gate_two_grad = jnp.sum(upstream * branch_two, axis=1)
    result = (middle + gate_two * branch_two).astype(BF16)
    for s in feed_sums:
        s.first()
    attended_grad = after(attended_grad, *[s.give for s in feed_sums])
    late_halves = sum_modes([gate_one_grad, shift_two_grad, scale_two_grad, gate_two_grad])
    place = lax.axis_index("y").astype(jnp.int32)
    scores_grad, query_grad, key_grad, value_grad, keep, give = attend_back(
        place.reshape(1), probs, queries, attended_grad, keys, values, mask, factor
    )
    kept_sent = project_back(
        in_turned, all_turned, out_turned, query_grad, key_grad.reshape(-1, width), value_grad.reshape(-1, width),
        logits_grad, branch_one_grad,
    )
    kept_sent = [split(v) for v in kept_sent]
    in_sums = [Reduction(tuple(kept_sent[3 * k : 3 * k + 2]), kept_sent[3 * k + 2], nz, routes[k]) for k in range(2)]
    got = swap(give, "y")
    pair_sums = (jnp.zeros((TILE, pair.shape[3]), F32),)
    steps_all = chains * (local // TILE) // 2
    quarter = steps_all // 4

    def more_pair(start, count, *needed):
        new_grad, new_sum = pair_back(after(scores_grad, *needed), pair, tall_pair, turn, start, count, *pair_sums)
        return (new_sum, new_grad)

    late_modes = share_modes(*late_halves, kept_sent[0])
    pair_sums = more_pair(0, quarter, kept_sent[0])
    for s in feed_sums:
        s.got = after(s.got, pair_sums[0])
        s.second()
    pair_sums = more_pair(quarter, quarter, *[s.give for s in feed_sums])
    late_modes = after(late_modes, pair_sums[0])
    for s in in_sums:
        s.got = after(s.got, pair_sums[0])
        s.first()
    owned = add_low(keep, after(got, *[s.give for s in in_sums])).reshape(rows, 2 * width)
    normed_one_grad = (
        dot(query_grad, first_w[:, :width], NT)
        + dot(owned[:, :width], first_w[:, width : 2 * width], NT)
        + dot(owned[:, width:], second_w[:, :width], NT)
        + dot(logits_grad, second_w[:, width : 2 * width], NT)
    ).reshape(chains, local, width)
    shift_one_grad = jnp.sum(normed_one_grad, axis=1)
    scale_one_grad = jnp.sum(normed_one_grad * norm_one, axis=1)
    early_halves = sum_modes([shift_one_grad, scale_one_grad])
    for s in feed_sums:
        s.got = after(s.got, normed_one_grad)
    feed_line = Line([s.third() for s in feed_sums], nz)
    early_modes = share_modes(*early_halves, feed_line.sent)
    for s in in_sums:
        s.got = after(s.got, feed_line.sent)
        s.second()
    pair_sums = more_pair(2 * quarter, quarter, feed_line.sent, *early_halves, *[s.give for s in in_sums])
    feed_line.got = after(feed_line.got, pair_sums[0])
    feed_line.next()
    for s in in_sums:
        s.got = after(s.got, feed_line.sent)
    in_line = Line([s.third() for s in in_sums], nz)
    pair_sums = more_pair(3 * quarter, steps_all - 3 * quarter, in_line.sent)
    tokens_grad = (middle_grad + normalise_back(normed_one_grad, scale_one, norm_one, root_one)).astype(BF16)
    early_modes = after(early_modes, pair_sums[0]).reshape(ndp * chains, -1)
    late_modes = late_modes.reshape(ndp * chains, -1)
    pair_w_sum, pair_grad = pair_sums
    grad_pair_w = pair_w_sum[:heads].T

    low_f32, ada_f32 = condition_low.astype(F32), w_ada.astype(F32)
    exact = lambda left, right, dims: lax.dot_general(left, right, (dims, ((), ())), precision=HIGH)
    cut = 2 * width
    grad_ada = jnp.concatenate([exact(low_f32, early_modes, TN), exact(low_f32, late_modes, TN)], axis=1)
    condition_grad = exact(early_modes, ada_f32[:, :cut], NT) + exact(late_modes, ada_f32[:, cut:], NT)
    before_grad = condition_grad * (sig_before * (1.0 + before * (1.0 - sig_before)))
    outer = lambda left: lax.dot_general(left.astype(F32), before_grad, (((0,), (0,)), ((), ())), precision=HIGH)
    grad_class, grad_arch, grad_topo = outer(hot[0]), outer(hot[1]), outer(hot[2])
    time_pack = jnp.concatenate(
        [outer(features).reshape(devices, time_rows * own), grad_pair_w.reshape(devices, -1)], axis=1
    )
    time_got = lax.all_to_all(time_pack, ALL, split_axis=0, concat_axis=0, tiled=True)
    in_line.got = after(in_line.got, time_pack)
    in_line.next()
    feed_total = feed_line.total(in_line.sent)
    early, late = jnp.split(feed_total, 2, axis=1)
    sum_gate, sum_up = early[:, :hidden_width], late[:, :hidden_width]
    sum_down = jnp.concatenate(
        [t[:, hidden_width + k * width : hidden_width + (k + 1) * width] for t in (early, late) for k in range(groups // 2)], axis=0
    )
    in_total = in_line.total(feed_total)
    time_got = after(time_got, in_total)
    sums = jnp.split(in_total, 2, axis=1)
    sum_out = jnp.concatenate([s[:, 2 * width :] for s in sums], axis=1)
    grad_time = time_got[:, :size_time].reshape(devices, time_rows, own).transpose(1, 0, 2).reshape(time_rows, width)
    grad_pair_own = jnp.sum(time_got[:, size_time:], axis=0).reshape(w_pair.shape)

    return (
        result,
        tokens_grad,
        pair_grad,
        grad_class,
        grad_arch,
        grad_topo,
        grad_time,
        grad_ada,
        jnp.concatenate([sums[0][:, : 2 * width], sums[1][:, :width]], axis=1),
        sums[1][:, width : 2 * width],
        sum_out,
        grad_pair_own,
        sum_gate,
        sum_up,
        sum_down,
    )


def solution(mesh):
    ndp, ny = mesh.shape["dp"], mesh.shape["seq"]
    sizes = (ndp // 4, 2, 2, ny)
    fine = Mesh(mesh.devices.reshape(sizes), ALL)
    row, col = P(ALL, None), P(None, ALL)
    in_specs = (P(DP, "y", None), P(DP, "y", None, None), P(DP), P(DP), P(DP), P(DP), P(DP, "y", None)) + (col,) * 3 + (row,) * 9
    out_specs = (P(DP, "y", None), P(DP, "y", None), P(DP, "y", None, None)) + (col,) * 3 + (row,) * 9

    def body(*args):
        return on_device(sizes, *args)

    return jax.shard_map(body, mesh=fine, in_specs=in_specs, out_specs=out_specs, check_vma=False)
```

```python
import functools
import math

import jax
import jax.numpy as jnp
from jax import lax
from jax.experimental import pallas as pl
from jax.experimental.pallas import tpu as pltpu
from jax.sharding import Mesh
from jax.sharding import PartitionSpec as P

EPSILON = 1e-06
TIME_SCALE = 100.0
F32 = jnp.float32
BF16 = jnp.bfloat16
DP = ("z", "x", "c")
ALL = ("z", "x", "c", "y")
HIGH = lax.Precision.HIGHEST
NT, TN = ((1,), (1,)), ((0,), (0,))
TILE = 16
VMEM = 60 * 1024 * 1024


def dot(left, right, dims=((1,), (0,))):
    return lax.dot_general(left, right, (dims, ((), ())), preferred_element_type=F32)


def params():
    return pltpu.CompilerParams(vmem_limit_bytes=VMEM)


def time_features(moment, width):
    half_width = width // 2
    frequency = jnp.exp(-math.log(10000.0) * jnp.arange(half_width, dtype=F32) / half_width)
    angles = TIME_SCALE * moment[:, None] * frequency[None, :]
    return jnp.concatenate([jnp.sin(angles), jnp.cos(angles)], axis=-1)


def normalise(rows):
    centre = rows - jnp.mean(rows, axis=-1, keepdims=True)
    spread = jnp.mean(centre * centre, axis=-1, keepdims=True)
    root = lax.rsqrt(spread + EPSILON)
    return centre * root, root


def normalise_back(grad, scale, normed, root):
    u = grad * (1.0 + scale)
    inner = u - jnp.mean(u, axis=-1, keepdims=True)
    return root * (inner - normed * jnp.mean(u * normed, axis=-1, keepdims=True))


def swap(value, axis):
    return lax.ppermute(value, axis, [(0, 1), (1, 0)])


def shift(value, axis, size, by):
    return lax.ppermute(value, axis, [(i, (i + by) % size) for i in range(size)])


def add_low(left, right):
    return (left.astype(F32) + right.astype(F32)).astype(BF16)


def after(value, *others):
    return lax.optimization_barrier((value, *others))[0]


def ordered(own, other, axis, at):
    low = jnp.stack([own, other], axis=at)
    high = jnp.stack([other, own], axis=at)
    return jnp.where(lax.axis_index(axis) == 0, low, high)


class Gathering:
    def __init__(self, block, nz, routes):
        self.nz, self.routes, self.block = nz, routes, block
        self.got = [shift(block, "z", nz, by) for by in range(1, nz)]

    def first(self):
        nz = self.nz
        parts = [self.block] + self.got
        line = jnp.stack([parts[(nz - 1 - i) % nz] for i in range(2 * nz - 1)])
        full = lax.dynamic_slice_in_dim(line, nz - 1 - lax.axis_index("z"), nz, 0)
        half = full.shape[-1] // 2
        self.full = [full[..., :half], full[..., half:]]
        self.got = [swap(f, r[0]) for f, r in zip(self.full, self.routes)]

    def second(self):
        self.full = [ordered(f, g, r[0], 1) for f, g, r in zip(self.full, self.got, self.routes)]
        self.got = [swap(f, r[1]) for f, r in zip(self.full, self.routes)]

    def third(self):
        self.full = [ordered(f, g, r[1], 2 if r[1] == "y" else 1) for f, g, r in zip(self.full, self.got, self.routes)]
        self.got = [swap(f, "c") for f in self.full]

    def total(self):
        return [ordered(f, g, "c", 2).reshape(-1, f.shape[-1]) for f, g in zip(self.full, self.got)]


def spread(rows, order, nz):
    n = 8 * nz * rows
    new = jnp.arange(n, dtype=jnp.int32)
    part = new // (nz * rows)
    at = {"c": part // 4, order[0]: part // 2 % 2, order[1]: part % 2}
    at = {k: v ^ lax.axis_index(k) for k, v in at.items()}
    old = (((new // rows % nz * 2 + at["x"]) * 2 + at["c"]) * 2 + at["y"]) * rows + new % rows
    return (jnp.arange(n, dtype=jnp.int32)[:, None] == old[None, :]).astype(BF16)


def down_order(rows, groups, routes, nz):
    n = 8 * nz * rows * groups
    new = jnp.arange(n, dtype=jnp.int32)
    group = new // (8 * nz * rows)
    part = new // (nz * rows) % 8
    late = group >= groups // 2
    firsts, seconds = part // 2 % 2, part % 2
    at = {"c": part // 4}
    for axis in ("x", "y"):
        early_bit = firsts if routes[1][0] == axis else seconds
        late_bit = firsts if routes[0][0] == axis else seconds
        at[axis] = jnp.where(late, late_bit, early_bit)
    at = {k: v ^ lax.axis_index(k) for k, v in at.items()}
    old = (((new // rows % nz * 2 + at["x"]) * 2 + at["c"]) * 2 + at["y"]) * groups * rows + group * rows + new % rows
    return (jnp.arange(n, dtype=jnp.int32)[None, :] == old[:, None]).astype(BF16)


def relative(value, hot):
    return dot(hot, value, ((0,), (1,))).astype(BF16)


class Reduction:
    def __init__(self, keep, send, nz, order):
        self.keep = keep if isinstance(keep, tuple) else (keep[:2], keep[2:])
        self.nz, self.order = nz, order
        self.got = swap(send, "c")

    def first(self):
        self.give = add_low(self.keep[1], self.got[2:])
        self.keep = add_low(self.keep[0], self.got[:2])
        self.got = swap(self.give, self.order[0])
        return self

    def second(self):
        self.give = add_low(self.keep[1], self.got[1])
        self.keep = add_low(self.keep[0], self.got[0])
        self.got = swap(self.give, self.order[1])
        return self

    def third(self):
        return add_low(self.keep, self.got)


class Line:
    def __init__(self, blocks, nz):
        block = jnp.concatenate(blocks, axis=-1)
        place = lax.axis_index("z")
        self.nz, self.by = nz, 1
        pick = lambda m: lax.dynamic_index_in_dim(block, place ^ m, 0, keepdims=False)
        self.keep = jnp.stack([pick(m) for m in range(0, nz, 2)])
        self.send(jnp.stack([pick(m) for m in range(1, nz, 2)]))

    def send(self, sent):
        self.sent = sent
        self.got = lax.ppermute(sent, "z", [(i, i ^ self.by) for i in range(self.nz)])

    def next(self):
        while self.by * 2 < self.nz:
            self.by *= 2
            total = add_low(self.keep, self.got)
            self.keep = total[::2]
            self.send(total[1::2])

    def total(self, *needed):
        got = after(self.got, *needed)
        return (self.keep.astype(F32) + got.astype(F32))[0]


def bias_kernel(pair_ref, wide_ref, out_ref):
    wide = wide_ref[...]
    lanes = lax.broadcasted_iota(jnp.int32, (pair_ref.shape[2], wide.shape[1]), 1) % TILE
    for n in range(out_ref.shape[1]):
        total = dot(pair_ref[0, n * TILE], wide)
        for i in range(1, TILE):
            total = jnp.where(lanes == i, dot(pair_ref[0, n * TILE + i], wide), total)
        out_ref[0, n] = total.T


def pair_bias(pair, wide, group=4):
    chains, local, length, channels = pair.shape
    blocks, tall = local // TILE, wide.shape[1]
    return pl.pallas_call(
        bias_kernel,
        grid=(chains, blocks // group),
        in_specs=[
            pl.BlockSpec((1, group * TILE, length, channels), lambda b, i: (b, i, 0, 0)),
            pl.BlockSpec(wide.shape, lambda b, i: (0, 0)),
        ],
        out_specs=pl.BlockSpec((1, group, tall, length), lambda b, i: (b, i, 0, 0)),
        out_shape=jax.ShapeDtypeStruct((chains, blocks, tall, length), F32),
        compiler_params=params(),
        cost_estimate=pl.CostEstimate(flops=2 * pair.size * tall, bytes_accessed=2 * pair.size, transcendentals=0),
        name="pair_bias",
    )(pair, wide)


def widen(ref, mask):
    heads, tiles = mask.shape[0] // TILE, ref.shape[0] // TILE
    return jnp.concatenate(
        [jnp.concatenate([ref[n * TILE : (n + 1) * TILE, :]] * heads, axis=0) * mask for n in range(tiles)], axis=0
    )


def narrow(mixed, mask):
    tall = mask.shape[0]
    mask = mask.astype(F32)
    rows = []
    for n in range(mixed.shape[0] // tall):
        own = mixed[n * tall : (n + 1) * tall] * mask
        total = own[:TILE]
        for h in range(1, tall // TILE):
            total = total + own[h * TILE : (h + 1) * TILE]
        rows.append(total)
    return jnp.concatenate(rows, axis=0)


def attend_kernel(factor, bias_ref, q_ref, k_ref, v_ref, mask_ref, probs_ref, out_ref):
    mask = mask_ref[...]
    shape = bias_ref.shape[1:]
    bias = bias_ref[0].reshape(-1, shape[-1])
    scores = dot(widen(q_ref, mask), k_ref[0], NT) * factor + bias
    powers = jnp.exp(scores - jnp.max(scores, axis=-1, keepdims=True))
    probs = powers * (1.0 / jnp.sum(powers, axis=-1, keepdims=True))
    probs_ref[0] = probs.reshape(shape)
    out_ref[...] = narrow(dot(probs.astype(BF16), v_ref[0]), mask)


def attend(bias, queries, keys, values, mask, factor, group=4):
    chains, blocks, tall, length = bias.shape
    width = mask.shape[1]
    rows = chains * blocks * TILE
    steps = blocks // group
    row_spec = pl.BlockSpec((group * TILE, width), lambda b, i: (b * steps + i, 0))
    square = pl.BlockSpec((1, group, tall, length), lambda b, i: (b, i, 0, 0))
    return pl.pallas_call(
        functools.partial(attend_kernel, factor),
        grid=(chains, steps),
        in_specs=[
            square,
            row_spec,
            pl.BlockSpec((1, length, width), lambda b, i: (b, 0, 0)),
            pl.BlockSpec((1, length, width), lambda b, i: (b, 0, 0)),
            pl.BlockSpec(mask.shape, lambda b, i: (0, 0)),
        ],
        out_specs=[square, row_spec],
        out_shape=[jax.ShapeDtypeStruct(bias.shape, F32), jax.ShapeDtypeStruct((rows, width), F32)],
        compiler_params=params(),
        cost_estimate=pl.CostEstimate(flops=4 * bias.size * width, bytes_accessed=10 * bias.size, transcendentals=bias.size),
        name="attend",
    )(bias, queries, keys, values, mask)


def attend_back_kernel(factor, place_ref, probs_ref, q_ref, g_ref, k_ref, v_ref, mask_ref, ds_ref, dq_ref, dk_ref, dv_ref,
                       keep_ref, give_ref, dk_sum, dv_sum):
    keys, values, mask = k_ref[0], v_ref[0], mask_ref[...]

    @pl.when(pl.program_id(1) == 0)
    def _():
        dk_sum[...] = jnp.zeros_like(dk_sum)
        dv_sum[...] = jnp.zeros_like(dv_sum)

    shape = probs_ref.shape[1:]
    probs = probs_ref[0].reshape(-1, shape[-1])
    queries, grads = widen(q_ref, mask), widen(g_ref, mask)
    probs_grad = dot(grads, values, NT)
    inner = jnp.sum(probs_grad * probs, axis=-1, keepdims=True)
    scores_grad = (probs * (probs_grad - inner)).astype(BF16)
    ds_ref[0] = scores_grad.reshape(shape)
    dq_ref[...] = (narrow(dot(scores_grad, keys), mask) * factor).astype(BF16)
    dk_sum[...] += dot(scores_grad, queries, TN)
    dv_sum[...] += dot(probs.astype(BF16), grads, TN)

    @pl.when(pl.program_id(1) == pl.num_programs(1) - 1)
    def _():
        dk_ref[0] = (dk_sum[...] * factor).astype(BF16)
        dv_ref[0] = dv_sum[...].astype(BF16)
        local = keep_ref.shape[1]
        for ref, place in ((keep_ref, place_ref[0]), (give_ref, 1 - place_ref[0])):
            at = pl.ds(pl.multiple_of(place * local, local), local)
            ref[0, :, : dk_sum.shape[1]] = (dk_sum[at, :] * factor).astype(BF16)
            ref[0, :, dk_sum.shape[1] :] = dv_sum[at, :].astype(BF16)


def attend_back(place, probs, queries, grads, keys, values, mask, factor, group=4):
    chains, blocks, tall, length = probs.shape
    width = mask.shape[1]
    rows = chains * blocks * TILE
    steps = blocks // group
    row_spec = pl.BlockSpec((group * TILE, width), lambda b, i: (b * steps + i, 0))
    square = pl.BlockSpec((1, group, tall, length), lambda b, i: (b, i, 0, 0))
    return pl.pallas_call(
        functools.partial(attend_back_kernel, factor),
        grid=(chains, steps),
        in_specs=[
            pl.BlockSpec(memory_space=pltpu.SMEM),
            square,
            row_spec,
            row_spec,
            pl.BlockSpec((1, length, width), lambda b, i: (b, 0, 0)),
            pl.BlockSpec((1, length, width), lambda b, i: (b, 0, 0)),
            pl.BlockSpec(mask.shape, lambda b, i: (0, 0)),
        ],
        out_specs=[square, row_spec] + [pl.BlockSpec((1, length, width), lambda b, i: (b, 0, 0))] * 2
        + [pl.BlockSpec((1, blocks * TILE, 2 * width), lambda b, i: (b, 0, 0))] * 2,
        out_shape=[
            jax.ShapeDtypeStruct(probs.shape, BF16),
            jax.ShapeDtypeStruct((rows, width), BF16),
            jax.ShapeDtypeStruct((chains, length, width), BF16),
            jax.ShapeDtypeStruct((chains, length, width), BF16),
            jax.ShapeDtypeStruct((chains, blocks * TILE, 2 * width), BF16),
            jax.ShapeDtypeStruct((chains, blocks * TILE, 2 * width), BF16),
        ],
        scratch_shapes=[pltpu.VMEM((length, width), F32), pltpu.VMEM((length, width), F32)],
        compiler_params=params(),
        cost_estimate=pl.CostEstimate(flops=10 * probs.size * width, bytes_accessed=6 * probs.size, transcendentals=0),
        name="attend_back",
    )(place, probs, queries, grads, keys, values, mask)


def pair_back_kernel(ds_ref, pair_ref, tall_ref, turn_ref, old_dw_ref, *rest):
    grad_ref, dw_ref = rest[-2:]

    @pl.when(pl.program_id(0) == 0)
    def _():
        dw_ref[...] = old_dw_ref[...]

    tall = tall_ref[...]
    total = dw_ref[...]
    for n in range(ds_ref.shape[1]):
        scores_grad = ds_ref[0, n]
        by_row = dot(turn_ref[...], scores_grad).astype(BF16)
        turned = scores_grad.T
        lanes = lax.broadcasted_iota(jnp.int32, turned.shape, 1) % TILE
        for i in range(TILE):
            at = n * TILE + i
            grad_ref[0, at] = dot(jnp.where(lanes == i, turned, jnp.zeros_like(turned)), tall).astype(BF16)
            total = total + dot(by_row[i * TILE : (i + 1) * TILE], pair_ref[0, at])
    dw_ref[...] = total


def pair_back(scores_grad, pair, tall, turn, start, count, old_dw, *old, group=2):
    chains, local, length, channels = pair.shape
    blocks, high = scores_grad.shape[1:3]
    blocks = blocks // group
    place = lambda i: ((start + i) // blocks, (start + i) % blocks, 0, 0)
    size = pair.size * count // (chains * blocks)
    fixed = lambda i: (0, 0)
    return pl.pallas_call(
        pair_back_kernel,
        grid=(count,),
        in_specs=[
            pl.BlockSpec((1, group, high, length), place),
            pl.BlockSpec((1, group * TILE, length, channels), place),
            pl.BlockSpec(tall.shape, fixed),
            pl.BlockSpec(turn.shape, fixed),
            pl.BlockSpec((TILE, channels), fixed),
        ]
        + [pl.BlockSpec(memory_space=pl.ANY)] * len(old),
        out_specs=[
            pl.BlockSpec((1, group * TILE, length, channels), place),
            pl.BlockSpec((TILE, channels), fixed),
        ],
        out_shape=[jax.ShapeDtypeStruct(pair.shape, BF16), jax.ShapeDtypeStruct((TILE, channels), F32)],
        input_output_aliases={5: 0} if old else {},
        compiler_params=params(),
        cost_estimate=pl.CostEstimate(flops=4 * size * high, bytes_accessed=4 * size, transcendentals=0),
        name="pair_back",
    )(scores_grad, pair, tall, turn, old_dw, *old)


def feed_kernel(steps, rows_ref, turned_ref, g_ref, order_ref, line_ref, gate_ref, up_ref, down_ref,
                out_ref, back_ref, *rest):
    grads_refs, held = rest[:-1], rest[-1]
    step = pl.program_id(0)
    per = held.shape[4] // steps
    shape = grads_refs[0].shape

    @pl.when(step == 0)
    def _():
        out_ref[...] = jnp.zeros_like(out_ref)
        back_ref[...] = jnp.zeros_like(back_ref)

    @pl.when(step < steps)
    def _():
        rows, grads = rows_ref[...], g_ref[...]
        w_gate, w_up = gate_ref[...], up_ref[...]
        width = rows.shape[1]
        stack = [down_ref[:, k * width : (k + 1) * width] for k in range(down_ref.shape[1] // width)]
        w_down = dot(line_ref[...], jnp.concatenate(stack, axis=0)).astype(BF16)
        gate = dot(rows, w_gate)
        up = dot(rows, w_up)
        sig = jax.nn.sigmoid(gate)
        silu = gate * sig
        hidden = (silu * up).astype(BF16)
        out_ref[...] += dot(hidden, w_down)
        hidden_grad = dot(grads, w_down, NT)
        gate_grad = (hidden_grad * up * (sig + silu * (1.0 - sig))).astype(BF16)
        up_grad = (hidden_grad * silu).astype(BF16)
        back_ref[...] += dot(gate_grad, w_gate, NT) + dot(up_grad, w_up, NT)
        for k, right in enumerate((gate_grad, up_grad)):
            full = dot(turned_ref[k], right).reshape((2,) + shape).astype(BF16)
            grads_refs[2 * k][...] = full[0]
            grads_refs[2 * k + 1][...] = full[1]
        hidden_turned = dot(order_ref[...], hidden, NT).astype(BF16)
        full = dot(hidden_turned, grads)
        full = full.reshape(held.shape[:4] + (per,) + shape[2:3] + (width,)).astype(BF16)
        held[:, :, :, :, pl.ds(step * per, per)] = full

    for route in range(2):
        for n in range(held.shape[1]):
            @pl.when(step == steps + n)
            def _(route=route, n=n):
                grads_refs[2 * route][...] = held[route, n, 0]
                grads_refs[2 * route + 1][...] = held[route, n, 1]


def feed(rows, turned, grads, order, line, weights, nz):
    count, width = rows.shape
    hidden = weights.shape[1] // 3
    block = order.shape[0]
    steps = hidden // block
    groups = hidden // width
    own = width // (8 * nz)
    fixed = lambda m: (0, 0)
    last = steps - 1
    columns = hidden + groups // 2 * width
    halves = jax.ShapeDtypeStruct((4, nz, own, columns), BF16)
    return pl.pallas_call(
        functools.partial(feed_kernel, steps),
        grid=(steps + groups // 2,),
        in_specs=[
            pl.BlockSpec((count, width), fixed),
            pl.BlockSpec((2, width, count), lambda m: (0, 0, 0)),
            pl.BlockSpec((count, width), fixed),
            pl.BlockSpec((block, block), fixed),
            pl.BlockSpec((block, block), fixed),
            pl.BlockSpec((width, block), lambda m: (0, jnp.minimum(m, last))),
            pl.BlockSpec((width, block), lambda m: (0, steps + jnp.minimum(m, last))),
            pl.BlockSpec((width // steps, hidden), lambda m: (jnp.minimum(m, last), 2)),
        ],
        out_specs=[
            pl.BlockSpec((count, width), fixed),
            pl.BlockSpec((count, width), fixed),
            *[pl.BlockSpec((4, nz, own, block), lambda m: (0, 0, 0, m))] * 4,
        ],
        out_shape=[
            jax.ShapeDtypeStruct((count, width), F32),
            jax.ShapeDtypeStruct((count, width), F32),
            *[halves] * 4,
        ],
        scratch_shapes=[pltpu.VMEM((2, groups // 2, 2, 4, nz, own, width), BF16)],
        compiler_params=params(),
        cost_estimate=pl.CostEstimate(flops=24 * count * width * hidden, bytes_accessed=12 * width * hidden, transcendentals=count * hidden),
        name="feed",
    )(rows, turned, grads, order, line, weights, weights, weights)


def join_kernel(cuts, *refs):
    at = 0
    for which, start, size in cuts:
        piece = refs[which][:, start : start + size] if len(refs[which].shape) == 2 else refs[which][start]
        refs[-1][:, at : at + piece.shape[1]] = piece
        at += piece.shape[1]


def join(arrays, cuts):
    return pl.pallas_call(
        functools.partial(join_kernel, cuts),
        out_shape=jax.ShapeDtypeStruct((arrays[0].shape[0], sum(c[2] for c in cuts)), BF16),
        compiler_params=params(),
        name="join",
    )(*arrays)


def project_kernel(own_ref, all_ref, first_ref, second_ref, q_ref, k_ref, v_ref, gate_ref):
    width = own_ref.shape[1]
    own, every = own_ref[...], all_ref[...]
    q_ref[...] = dot(own, first_ref[:, :width]).astype(BF16)
    k_ref[...] = dot(every, first_ref[:, width : 2 * width]).astype(BF16)
    v_ref[...] = dot(every, second_ref[:, :width]).astype(BF16)
    gate_ref[...] = dot(own, second_ref[:, width : 2 * width])


def project(own, every, first, second):
    count, width = own.shape
    many = every.shape[0]
    return pl.pallas_call(
        project_kernel,
        out_shape=[
            jax.ShapeDtypeStruct((count, width), BF16),
            jax.ShapeDtypeStruct((many, width), BF16),
            jax.ShapeDtypeStruct((many, width), BF16),
            jax.ShapeDtypeStruct((count, width), F32),
        ],
        compiler_params=params(),
        cost_estimate=pl.CostEstimate(flops=4 * (count + many) * width * width, bytes_accessed=12 * width * width, transcendentals=0),
        name="project",
    )(own, every, first, second)


def project_back_kernel(own_ref, all_ref, gated_ref, dq_ref, dk_ref, dv_ref, dg_ref, out_ref, *sums):
    width = own_ref.shape[1]
    half = width // 2
    for k, (inner, outer) in enumerate((((own_ref, dq_ref), (all_ref, dk_ref)), ((all_ref, dv_ref), (own_ref, dg_ref)))):
        for n, rows in enumerate((slice(0, half // 2), slice(half // 2, half), slice(half, width))):
            result = sums[3 * k + n]
            result[:, :width] = dot(inner[0][k, rows], inner[1][...]).astype(BF16)
            result[:, width : 2 * width] = dot(outer[0][k, rows], outer[1][...]).astype(BF16)
            result[:, 2 * width :] = dot(gated_ref[k, rows], out_ref[:, k * half : (k + 1) * half]).astype(BF16)


def project_back(own, every, gated, dq, dk, dv, dg, out):
    width = own.shape[1]
    return pl.pallas_call(
        project_back_kernel,
        out_shape=[jax.ShapeDtypeStruct((width // n, 5 * width // 2), BF16) for n in (4, 4, 2)] * 2,
        compiler_params=params(),
        cost_estimate=pl.CostEstimate(flops=16 * own.size * width, bytes_accessed=16 * width * width, transcendentals=0),
        name="project_back",
    )(own, every, gated, dq, dk, dv, dg, out)


def on_device(sizes, tokens, pair, cath_class, cath_arch, cath_topo, times, out_grad,
              emb_class, emb_arch, emb_topo, w_time, w_ada, w_qkv, w_gate, w_out, w_pair,
              w_ffgate, w_ffup, w_ffdown):
    nz, nx, nc, ny = sizes
    ndp = nz * nx * nc
    devices = ndp * ny
    chains, local, width = tokens.shape
    length = pair.shape[2]
    heads = w_pair.shape[1]
    head = width // heads
    factor = head ** (-0.5)
    rows = chains * local
    own = emb_class.shape[1]
    hidden_width = w_ffgate.shape[1]
    time_rows = w_time.shape[0]

    half = width // 2
    groups = w_ffdown.shape[0] // own
    routes = (("y", "x"), ("x", "y"))
    stacked = join(
        (w_ffgate, w_ffup, w_ffdown.reshape(groups, own, width)),
        [(0, 0, hidden_width), (1, 0, hidden_width)] + [(2, k, width) for k in range(groups)],
    )
    weights = lax.all_gather(stacked, ALL, axis=0, tiled=True)
    packed = join(
        (w_qkv, w_gate, w_out),
        [(0, 0, 2 * width), (2, 0, half), (0, 2 * width, width), (1, 0, width), (2, half, half)],
    )
    attention = Gathering(packed, nz, routes)
    tokens_other = swap(tokens, "y")

    facts = jnp.stack([cath_class.astype(F32), cath_arch.astype(F32), cath_topo.astype(F32), times]).reshape(1, -1)
    pair_rows_w = w_pair.astype(F32).reshape(1, -1)
    pack = jnp.concatenate(
        [
            w_time.astype(F32).reshape(time_rows, devices, own).transpose(1, 0, 2).reshape(devices, -1),
            jnp.broadcast_to(facts, (devices, facts.shape[1])),
            jnp.broadcast_to(pair_rows_w, (devices, pair_rows_w.shape[1])),
        ],
        axis=1,
    )
    got = lax.all_to_all(pack, ALL, split_axis=0, concat_axis=0, tiled=True)
    size_time = time_rows * own
    time_columns = got[:, :size_time].reshape(devices * time_rows, own).astype(BF16)
    size_facts = 4 * chains
    everyone = got[:, size_time : size_time + size_facts].reshape(ndp, ny, 4, chains)[:, 0]
    everyone = everyone.transpose(1, 0, 2).reshape(4, ndp * chains)
    full_pair_w = got[:, size_time + size_facts :].reshape(-1, heads).astype(BF16)
    labels = everyone[:3].astype(jnp.int32)
    features = time_features(everyone[3], devices * time_rows).astype(BF16)
    hot = [
        (labels[k][:, None] == jnp.arange(table.shape[0], dtype=jnp.int32)[None, :]).astype(BF16)
        for k, table in enumerate((emb_class, emb_arch, emb_topo))
    ]
    before = dot(hot[0], emb_class) + dot(hot[1], emb_arch) + dot(hot[2], emb_topo) + dot(features, time_columns)
    sig_before = jax.nn.sigmoid(before)
    condition_low = (before * sig_before).astype(BF16)
    modes_part = dot(condition_low, w_ada)
    modes = lax.all_to_all(modes_part.reshape(ndp, chains, 6 * width), DP, split_axis=0, concat_axis=0, tiled=True)
    modes = jnp.sum(modes, axis=0)
    modes = modes + swap(modes, "y")
    shift_one, scale_one, gate_one, shift_two, scale_two, gate_two = (
        m[:, None, :] for m in jnp.split(modes, 6, axis=-1)
    )

    entry = tokens.astype(F32)
    norm_one, root_one = normalise(entry)
    normed_one = (norm_one * (1.0 + scale_one) + shift_one).astype(BF16)
    norm_other, _ = normalise(tokens_other.astype(F32))
    normed_other = (norm_other * (1.0 + scale_one) + shift_one).astype(BF16)
    normed_all = ordered(normed_one, normed_other, "y", 1).reshape(chains * length, width)
    normed_one = normed_one.reshape(rows, width)
    mask = (jnp.arange(heads * TILE)[:, None] // TILE == jnp.arange(width)[None, :] // head).astype(BF16)
    wide_pair = jnp.repeat(full_pair_w, TILE, axis=1)
    attention.first()
    bias = pair_bias(after(pair, *attention.full), wide_pair)
    attention.got[0] = after(attention.got[0], bias)
    attention.second()
    hots = [spread(own, route, nz) for route in routes]
    steps = hidden_width // width
    order = down_order(own, groups, routes, nz // steps)
    in_turned = jnp.stack([relative(normed_one, hot) for hot in hots])
    all_turned = jnp.stack([relative(normed_all, hot) for hot in hots])
    attention.third()
    first_w, second_w = attention.total()
    full_out = jnp.concatenate([first_w[:, 2 * width :], second_w[:, 2 * width :]], axis=1)
    queries, keys, values, gate_logits = project(normed_one, normed_all, first_w, second_w)
    keys, values = keys.reshape(chains, length, width), values.reshape(chains, length, width)
    sigmoid_gate = jax.nn.sigmoid(gate_logits)
    probs, attended = attend(bias, queries, keys, values, mask, factor)
    gated = (attended * sigmoid_gate).astype(BF16)
    branch_one = dot(gated, full_out).reshape(chains, local, width)
    middle = entry + gate_one * branch_one
    norm_two, root_two = normalise(middle)
    normed_two = (norm_two * (1.0 + scale_two) + shift_two).astype(BF16).reshape(rows, width)
    upstream = out_grad.astype(F32)
    branch_two_grad = (gate_two * upstream).astype(BF16).reshape(rows, width)
    out_turned = jnp.stack([relative(gated, hot) for hot in hots])
    turned = jnp.stack([relative(normed_two, hots[k]) for k in (1, 0)])
    new = jnp.arange(width, dtype=jnp.int32)
    per_step = width // (steps * own)
    old = (new // own % groups) * (per_step * own) + new // (groups * own) * own + new % own
    line = (jnp.arange(width, dtype=jnp.int32)[None, :] == old[:, None]).astype(BF16)
    turn_rows = jnp.arange(TILE * TILE)[:, None]
    turn_columns = jnp.arange(heads * TILE)[None, :]
    turn = ((turn_rows // TILE == turn_columns % TILE) & (turn_rows % TILE == turn_columns // TILE)).astype(BF16)
    tall_pair = wide_pair.T
    weights = after(weights, out_turned, turned, in_turned, all_turned, turn, tall_pair)
    branch_two, normed_two_grad, *grads = feed(normed_two, turned, branch_two_grad, order, line, weights, nz)
    feed_sums = [Reduction(grads[2 * k], grads[2 * k + 1], nz, routes[1 - k]) for k in range(2)]
    split = lambda v: v.reshape(-1, nz, own, v.shape[-1])

    def sum_modes(parts):
        mine = jnp.concatenate(parts, axis=-1)
        return mine, swap(mine, "y")

    def share_modes(mine, other, *needed):
        mine = mine + after(other, *needed)
        mine = jnp.broadcast_to(mine[None], (ndp,) + mine.shape)
        return lax.all_to_all(mine, DP, split_axis=0, concat_axis=0, tiled=True)

    normed_two_grad = normed_two_grad.reshape(chains, local, width)
    middle_grad = upstream + normalise_back(normed_two_grad, scale_two, norm_two, root_two)
    branch_one_grad = (gate_one * middle_grad).astype(BF16).reshape(rows, width)
    gated_grad = dot(branch_one_grad, full_out, NT)
    attended_grad = (gated_grad * sigmoid_gate).astype(BF16)
    logits_grad = (gated_grad * attended * (sigmoid_gate * (1.0 - sigmoid_gate))).astype(BF16)
    branch_two = branch_two.reshape(chains, local, width)
    gate_one_grad = jnp.sum(middle_grad * branch_one, axis=1)
    shift_two_grad = jnp.sum(normed_two_grad, axis=1)
    scale_two_grad = jnp.sum(normed_two_grad * norm_two, axis=1)
    gate_two_grad = jnp.sum(upstream * branch_two, axis=1)
    result = (middle + gate_two * branch_two).astype(BF16)
    for s in feed_sums:
        s.first()
    attended_grad = after(attended_grad, *[s.give for s in feed_sums])
    late_halves = sum_modes([gate_one_grad, shift_two_grad, scale_two_grad, gate_two_grad])
    place = lax.axis_index("y").astype(jnp.int32)
    scores_grad, query_grad, key_grad, value_grad, keep, give = attend_back(
        place.reshape(1), probs, queries, attended_grad, keys, values, mask, factor
    )
    kept_sent = project_back(
        in_turned, all_turned, out_turned, query_grad, key_grad.reshape(-1, width), value_grad.reshape(-1, width),
        logits_grad, branch_one_grad,
    )
    kept_sent = [split(v) for v in kept_sent]
    in_sums = [Reduction(tuple(kept_sent[3 * k : 3 * k + 2]), kept_sent[3 * k + 2], nz, routes[k]) for k in range(2)]
    got = swap(give, "y")
    pair_sums = (jnp.zeros((TILE, pair.shape[3]), F32),)
    steps_all = chains * (local // TILE) // 2
    quarter = steps_all // 4
    ahead = quarter + quarter // 2

    def more_pair(start, count, *needed):
        new_grad, new_sum = pair_back(after(scores_grad, *needed), pair, tall_pair, turn, start, count, *pair_sums)
        return (new_sum, new_grad)

    late_modes = share_modes(*late_halves, kept_sent[0])
    pair_sums = more_pair(0, ahead, kept_sent[0])
    for s in feed_sums:
        s.got = after(s.got, pair_sums[0])
        s.second()
    pair_sums = more_pair(ahead, 2 * quarter - ahead, *[s.give for s in feed_sums])
    late_modes = after(late_modes, pair_sums[0])
    for s in in_sums:
        s.got = after(s.got, pair_sums[0])
        s.first()
    owned = add_low(keep, after(got, *[s.give for s in in_sums])).reshape(rows, 2 * width)
    normed_one_grad = (
        dot(query_grad, first_w[:, :width], NT)
        + dot(owned[:, :width], first_w[:, width : 2 * width], NT)
        + dot(owned[:, width:], second_w[:, :width], NT)
        + dot(logits_grad, second_w[:, width : 2 * width], NT)
    ).reshape(chains, local, width)
    shift_one_grad = jnp.sum(normed_one_grad, axis=1)
    scale_one_grad = jnp.sum(normed_one_grad * norm_one, axis=1)
    early_halves = sum_modes([shift_one_grad, scale_one_grad])
    for s in feed_sums:
        s.got = after(s.got, normed_one_grad)
    feed_line = Line([s.third() for s in feed_sums], nz)
    early_modes = share_modes(*early_halves, feed_line.sent)
    for s in in_sums:
        s.got = after(s.got, feed_line.sent)
        s.second()
    pair_sums = more_pair(2 * quarter, quarter, feed_line.sent, *early_halves, *[s.give for s in in_sums])
    feed_line.got = after(feed_line.got, pair_sums[0])
    feed_line.next()
    for s in in_sums:
        s.got = after(s.got, feed_line.sent)
    in_line = Line([s.third() for s in in_sums], nz)
    pair_sums = more_pair(3 * quarter, steps_all - 3 * quarter, in_line.sent)
    tokens_grad = (middle_grad + normalise_back(normed_one_grad, scale_one, norm_one, root_one)).astype(BF16)
    early_modes = after(early_modes, pair_sums[0]).reshape(ndp * chains, -1)
    late_modes = late_modes.reshape(ndp * chains, -1)
    pair_w_sum, pair_grad = pair_sums
    grad_pair_w = pair_w_sum[:heads].T

    low_f32, ada_f32 = condition_low.astype(F32), w_ada.astype(F32)
    exact = lambda left, right, dims: lax.dot_general(left, right, (dims, ((), ())), precision=HIGH)
    cut = 2 * width
    grad_ada = jnp.concatenate([exact(low_f32, early_modes, TN), exact(low_f32, late_modes, TN)], axis=1)
    condition_grad = exact(early_modes, ada_f32[:, :cut], NT) + exact(late_modes, ada_f32[:, cut:], NT)
    before_grad = condition_grad * (sig_before * (1.0 + before * (1.0 - sig_before)))
    outer = lambda left: lax.dot_general(left.astype(F32), before_grad, (((0,), (0,)), ((), ())), precision=HIGH)
    grad_class, grad_arch, grad_topo = outer(hot[0]), outer(hot[1]), outer(hot[2])
    time_pack = jnp.concatenate(
        [outer(features).reshape(devices, time_rows * own), grad_pair_w.reshape(devices, -1)], axis=1
    )
    in_line.got = after(in_line.got, time_pack)
    in_line.next()
    time_pack = after(time_pack, in_line.sent)
    time_got = lax.all_to_all(time_pack, ALL, split_axis=0, concat_axis=0, tiled=True)
    feed_total = feed_line.total(in_line.sent)
    early, late = jnp.split(feed_total, 2, axis=1)
    sum_gate, sum_up = early[:, :hidden_width], late[:, :hidden_width]
    sum_down = jnp.concatenate(
        [t[:, hidden_width + k * width : hidden_width + (k + 1) * width] for t in (early, late) for k in range(groups // 2)], axis=0
    )
    in_total = in_line.total(feed_total)
    time_got = after(time_got, in_total)
    sums = jnp.split(in_total, 2, axis=1)
    sum_out = jnp.concatenate([s[:, 2 * width :] for s in sums], axis=1)
    grad_time = time_got[:, :size_time].reshape(devices, time_rows, own).transpose(1, 0, 2).reshape(time_rows, width)
    grad_pair_own = jnp.sum(time_got[:, size_time:], axis=0).reshape(w_pair.shape)

    return (
        result,
        tokens_grad,
        pair_grad,
        grad_class,
        grad_arch,
        grad_topo,
        grad_time,
        grad_ada,
        jnp.concatenate([sums[0][:, : 2 * width], sums[1][:, :width]], axis=1),
        sums[1][:, width : 2 * width],
        sum_out,
        grad_pair_own,
        sum_gate,
        sum_up,
        sum_down,
    )


def solution(mesh):
    ndp, ny = mesh.shape["dp"], mesh.shape["seq"]
    sizes = (ndp // 4, 2, 2, ny)
    fine = Mesh(mesh.devices.reshape(sizes), ALL)
    row, col = P(ALL, None), P(None, ALL)
    in_specs = (P(DP, "y", None), P(DP, "y", None, None), P(DP), P(DP), P(DP), P(DP), P(DP, "y", None)) + (col,) * 3 + (row,) * 9
    out_specs = (P(DP, "y", None), P(DP, "y", None), P(DP, "y", None, None)) + (col,) * 3 + (row,) * 9

    def body(*args):
        return on_device(sizes, *args)

    return jax.shard_map(body, mesh=fine, in_specs=in_specs, out_specs=out_specs, check_vma=False)
```
